128 devices in a mesh: lat: 8 (over z, core), lon: 16 (over x, y).
Axes of the slice: x: 4, y: 4, z: 4, core: 2. Of those that a mesh axis runs over, the one named last changes fastest.
Arguments:
- obs_values: bfloat16 [524288, 128], P(('lat', 'lon')), may hold values from -6 to 6
- obs_dest: int32 [524288, 1], P(('lat', 'lon')), may hold values from 0 to 127; in each aligned block of 4096 rows (0 to 4095, 4096 to 8191, ...) at most 64 rows name the same one
- obs_cell: int32 [524288], P(('lat', 'lon')), may hold values from 0 to 8191
- obs_count: int32 [128], P(('lat', 'lon')), may hold values from 1 to 4096, 458752 in all
- conv_in: bfloat16 [3, 3, 128, 256], replicated, may hold values from -0.1875 to 0.1875
- conv_down: bfloat16 [3, 3, 256, 256], replicated, may hold values from -0.125 to 0.125
Outputs:
- encoded: bfloat16 [128, 2048, 256], P('lat', 'lon')
The draws below stay inside these ranges and needn't reach their ends.
Inputs may be any that keep to these rules, and one draw needn't show every extreme that they name: `obs_dest`: within the rows of one device, no tile is named by more than 64 rows, and some device's rows name one tile exactly 64 times. `obs_count`: the counts sum to 458752 and the largest is 4096.
All inputs are finite; a program needn't handle non-finite values.
Results may differ from the reference program's by a relative error of at most 0.0052.
Values may be sent and summed in bfloat16 or wider, within the bound.
No kernel may reach another device: no remote copies, remote signals or barrier semaphores. Data moves between devices by JAX's collectives and lax.ppermute only.
A program may use at most 64 MiB of HBM per device.

```python
import math
import jax
import jax.numpy as jnp
import numpy as np
from jax import lax

CH = 128
HID = 256
TH = 32
TW = 256
OBS_DEV = 4096
CAP = 64
NLAT = 256
NLON = 4096
OBS = 524288
DEVICES = 128


def plant(entries, key, least, largest):
    shape = entries.shape
    spot = [jax.random.randint(jax.random.fold_in(key, axis), (), 0, shape[axis]) for axis in range(len(shape))]
    entries = entries.at[tuple(spot)].set(least)
    longest = shape.index(max(shape))
    spot[longest] = (spot[longest] + 1) % shape[longest]
    return entries.at[tuple(spot)].set(largest)


def steps_of(own_key, shape, cuts, smallest, high):
    loudness = 1.0
    for dim, blocks in cuts:
        heights = jax.random.uniform(jax.random.fold_in(jax.random.fold_in(own_key, 6), dim), (blocks,), jnp.float32, smallest / len(cuts), high / len(cuts))
        loudness = loudness * jnp.repeat(jnp.exp(heights), shape[dim] // blocks).reshape((-1,) + (1,) * (len(shape) - 1 - dim))
    return loudness


def split_up(number_of, total, reach, skew):
    portions = [(1 << 20) // math.isqrt(standing ** skew) + 1 for standing in range(2, number_of + 1)]
    rest, holding = total - reach - (number_of - 1), [1] * (number_of - 1)
    while rest > 0:
        movable = [i for i in range(number_of - 1) if holding[i] < reach]
        mass, left = sum([portions[i] for i in movable]), rest
        for i in movable:
            addition = min(reach - holding[i], max(1, left * portions[i] // mass), rest)
            holding[i] = holding[i] + addition
            rest = rest - addition
    return np.array([reach] + holding)


def uneven(stream_key, count, total, limit, lean):
    if count == 2:
        one = jax.random.randint(stream_key, (), max(1, total - limit), min(limit, total - 1) + 1)
        return jnp.stack([one, total - one])
    tallies = jnp.asarray(split_up(count, total, limit, lean), jnp.int32)
    twos = (count - 1) // 2
    source_of, sink = tallies[1:1 + 2 * twos:2], tallies[2:2 + 2 * twos:2]
    margin = jnp.minimum(source_of - 1, limit - sink)
    passed = jax.random.randint(jax.random.fold_in(stream_key, 1), (twos,), 0, 1 << 20) % (margin + 1)
    tallies = tallies.at[1:1 + 2 * twos:2].set(source_of - passed).at[2:2 + 2 * twos:2].set(sink + passed)
    return tallies[jax.random.permutation(jax.random.fold_in(stream_key, 2), count)]


def shared_out(stream_key, own, number, rows, count, top, bound, slope):
    order = jax.random.permutation(stream_key, count)
    heavy_load, common = shares(count, rows * top, bound, slope, True), shares(count, rows * top, bound, slope, False)
    places = jnp.arange(count)

    def named(sizes, rotation):
        used = int((sizes > 0).sum())
        fixed = max(1, used // 4)
        moved = fixed + (places - fixed + rotation * (used - fixed)) % max(1, count - fixed)
        return jnp.zeros((count,), jnp.int32).at[order[jnp.where(places < fixed, places, moved)]].set(jnp.asarray(sizes, jnp.int32))

    sizes = jnp.where(number % 4 == 0, named(heavy_load, number // 4), named(common, number - number // 4 - 1))
    mixed = jax.random.permutation(jax.random.fold_in(own, 3), count)
    donor, receiver = mixed[0:count // 2 * 2:2], mixed[1:count // 2 * 2:2]
    margin = jnp.minimum(sizes[donor] - 1, bound - sizes[receiver]) // 2
    margin = jnp.where((donor == order[0]) | (receiver == order[0]) | (sizes[receiver] == 0), 0, jnp.maximum(margin, 0))
    moved = jax.random.randint(jax.random.fold_in(own, 4), (count // 2,), 0, 1 << 20) % (margin + 1)
    sizes = sizes.at[donor].add(-moved).at[receiver].add(moved)
    labels = jnp.searchsorted(jnp.cumsum(sizes), jnp.arange(rows * top), side="right").astype(jnp.int32)
    table = labels.reshape(top, rows).T
    table = table[jax.random.permutation(jax.random.fold_in(own, 1), rows)]
    rotation = jax.random.randint(jax.random.fold_in(own, 2), (rows, 1), 0, top)
    return jnp.take_along_axis(table, (jnp.arange(top)[None, :] + rotation) % top, axis=1)


def shares(number_of, total, limit, skew, full):
    portions = [(1 << 20) // math.isqrt(rank ** skew) + 1 for rank in range(1, number_of + 1)]
    largest = limit if full else min(limit, max(-(-total // number_of), total * portions[0] // sum(portions)))
    least = 1 if total - largest >= number_of - 1 else 0
    given, rest = [largest] + [least] * (number_of - 1), total - largest - least * (number_of - 1)
    while rest > 0:
        free = [i for i in range(1, number_of) if given[i] < largest] or [i for i in range(1, number_of) if given[i] < limit]
        mass, left = sum([portions[i] for i in free]), rest
        for i in free:
            extra = min(limit - given[i], max(1, left * portions[i] // mass), rest)
            given[i] = given[i] + extra
            rest = rest - extra
    return np.array(given)


def noise(rng, shape, scale, most, shards=(), kind=jnp.bfloat16):
    gain = steps_of(rng, shape, shards, -0.22, 0.18) if shards else 1.0
    entries = jax.random.normal(rng, shape, jnp.float32) * scale * gain
    return jnp.minimum(jnp.maximum(entries, -most), most).astype(kind)


def setup_inputs(seed: int = 0) -> dict:
    streams_of = jax.random.split(jax.random.key(seed), 7)
    obs_values = noise(streams_of[0], (OBS, CH), 1.0, 6.0, ((0, 128),))
    obs_dest_keys = jax.random.split(jax.random.fold_in(streams_of[1], 1), OBS // OBS_DEV)
    obs_dest_turns = jax.random.permutation(jax.random.fold_in(streams_of[1], 3), OBS // OBS_DEV)
    obs_dest = jax.vmap(lambda own, number: shared_out(jax.random.fold_in(streams_of[1], 2), own, number, OBS_DEV, DEVICES, 1, CAP, 2))(obs_dest_keys, obs_dest_turns).reshape((OBS, 1))
    obs_cell = plant(jax.random.randint(streams_of[2], (OBS,), 0, TH * TW), jax.random.fold_in(streams_of[2], 1), 0, (TH * TW) - 1).astype(jnp.int32)
    obs_count = uneven(streams_of[3], DEVICES, DEVICES * OBS_DEV * 7 // 8, OBS_DEV, 1).astype(jnp.int32)
    conv_in = noise(streams_of[4], (3, 3, CH, HID), (9 * CH) ** -0.5, 0.1875)
    conv_down = noise(streams_of[5], (3, 3, HID, HID), (9 * HID) ** -0.5, 0.125)
    return {"obs_values": obs_values, "obs_dest": obs_dest, "obs_cell": obs_cell, "obs_count": obs_count, "conv_in": conv_in, "conv_down": conv_down}


def convolve(field, weights, stride):
    return lax.conv_general_dilated(field[None], weights, (stride, stride), "VALID", dimension_numbers=("NHWC", "HWIO", "NHWC"), preferred_element_type=jnp.float32)[0]


def pad_field(field):
    padded = jnp.pad(field, ((1, 1), (0, 0), (0, 0)))
    return jnp.concatenate([padded[:, -1:], padded, padded[:, :1]], axis=1)


def reference(obs_values, obs_dest, obs_cell, obs_count, conv_in, conv_down):
    total_rows = obs_values.shape[0]
    row_ids = jnp.arange(total_rows, dtype=jnp.int32)
    source_ids = row_ids // OBS_DEV
    is_valid = (row_ids % OBS_DEV) < obs_count[source_ids]
    target = obs_dest[:, 0]
    sectors = NLON // TW
    lat_cell = (target // sectors) * TH + obs_cell // TW
    lon_cell = (target % sectors) * TW + obs_cell % TW
    flat_cell = jnp.where(is_valid, lat_cell * NLON + lon_cell, NLAT * NLON).astype(jnp.int32)
    cell_sums = jax.ops.segment_sum(obs_values.astype(jnp.float32), flat_cell, NLAT * NLON + 1)[:-1]
    cell_counts = jax.ops.segment_sum(jnp.ones((total_rows,), jnp.float32), flat_cell, NLAT * NLON + 1)[:-1]
    gridded = (cell_sums / jnp.maximum(cell_counts, 1.0)[:, None]).astype(jnp.bfloat16).reshape(NLAT, NLON, CH)
    hidden = jax.nn.gelu(convolve(pad_field(gridded), conv_in, 1)).astype(jnp.bfloat16)
    return jax.nn.gelu(convolve(pad_field(hidden), conv_down, 2)).astype(jnp.bfloat16)
```

```python
import functools

import jax
import jax.numpy as jnp
from jax import lax
from jax.experimental import pallas as pl
from jax.experimental.pallas import tpu as pltpu
from jax.sharding import PartitionSpec as P

TH = 32
TW = 256
CH = 128
HID = 256
DEV = 128
CAP = 64
ROWS = 4096
BLK = 72
SEND = DEV * BLK
TRASH = 256
GROUP = 32
COLS = 48
F32 = jnp.float32
BF16 = jnp.bfloat16


def gelu(x):
    inner = x * (0.7978845608028654 + 0.035677408136300125 * (x * x))
    return (0.5 * x) * (1.0 + jnp.tanh(inner))


def pack_kernel(count_ref, dest_ref, cell_ref, val_ref, out_ref, x32, o32, slot_v, slot_s, sem):
    count = count_ref[0]
    lane = lax.broadcasted_iota(jnp.int32, (1, 256), 1)
    dest_ids = lax.broadcasted_iota(jnp.int32, (DEV, 256), 0)
    pos_ids = lax.broadcasted_iota(jnp.int32, (CAP, 256), 0)
    upper = (
        lax.broadcasted_iota(jnp.int32, (256, 256), 0)
        < lax.broadcasted_iota(jnp.int32, (256, 256), 1)
    ).astype(F32).astype(BF16)
    carry = jnp.zeros((DEV, 1), F32)
    cells = jnp.zeros((DEV, 2 * CAP), F32)
    for a in range(ROWS // 256):
        dest = jnp.concatenate([dest_ref[2 * a : 2 * a + 1], dest_ref[2 * a + 1 : 2 * a + 2]], axis=1)
        cell = jnp.concatenate([cell_ref[2 * a : 2 * a + 1], cell_ref[2 * a + 1 : 2 * a + 2]], axis=1)
        live = (lane + 256 * a) < count
        dest_or = jnp.where(live, dest, DEV)
        hot = (dest_ids == dest_or).astype(F32)
        hot16 = hot.astype(BF16)
        before = jnp.dot(hot16, upper, preferred_element_type=F32) + carry
        carry = carry + jnp.sum(hot, axis=1, keepdims=True)
        pos = jnp.sum(hot * before, axis=0, keepdims=True).astype(jnp.int32)
        slot = jnp.where(live, dest * BLK + pos, SEND)
        slot_v[2 * a : 2 * a + 1] = slot[:, :128]
        slot_v[2 * a + 1 : 2 * a + 2] = slot[:, 128:]
        high = (cell // TW + 1).astype(F32)
        low = ((cell % 16) * 16 + (cell % TW) // 16).astype(F32)
        pos_hot = pos_ids == pos
        coded = jnp.concatenate(
            [jnp.where(pos_hot, high, 0.0), jnp.where(pos_hot, low, 0.0)], axis=0
        ).astype(BF16)
        cells = cells + lax.dot_general(
            hot16, coded, (((1,), (1,)), ((), ())), preferred_element_type=F32
        )
    to_scalar = pltpu.make_async_copy(slot_v, slot_s, sem)
    to_scalar.start()

    def widen(i, c):
        rows = pl.ds(pl.multiple_of(i * 128, 128), 128)
        x32[rows, :] = val_ref[rows, :].astype(F32)
        return c

    lax.fori_loop(0, ROWS // 128, widen, 0)
    to_scalar.wait()

    def move(i, c):
        for k in range(32):
            slot = slot_s[i // 4, (i % 4) * 32 + k]
            o32[pl.ds(slot, 1), :] = x32[pl.ds(i * 32 + k, 1), :]
        return c

    lax.fori_loop(0, ROWS // 32, move, 0)
    for d in range(DEV):
        o32[d * BLK + CAP : d * BLK + CAP + 1, :] = cells[d : d + 1, :]

    def narrow(i, c):
        rows = pl.ds(pl.multiple_of(i * 128, 128), 128)
        out_ref[rows, :] = o32[rows, :].astype(BF16)
        return c

    lax.fori_loop(0, SEND // 128, narrow, 0)


def pack(obs_values, obs_dest, obs_cell, obs_count):
    return pl.pallas_call(
        pack_kernel,
        out_shape=jax.ShapeDtypeStruct((SEND, CH), BF16),
        in_specs=[pl.BlockSpec(memory_space=pltpu.SMEM)] + [pl.BlockSpec(memory_space=pltpu.VMEM)] * 3,
        out_specs=pl.BlockSpec(memory_space=pltpu.VMEM),
        scratch_shapes=[
            pltpu.VMEM((ROWS, CH), F32),
            pltpu.VMEM((SEND + 8, CH), F32),
            pltpu.VMEM((32, 128), jnp.int32),
            pltpu.SMEM((32, 128), jnp.int32),
            pltpu.SemaphoreType.DMA,
        ],
        compiler_params=pltpu.CompilerParams(vmem_limit_bytes=40 * 1024 * 1024),
        name="pack",
    )(obs_count, obs_dest.reshape(32, 128), obs_cell.reshape(32, 128), obs_values)


def grid_kernel(
    got_ref, out_ref, top_ref, bottom_ref, edge_ref, x32, acc, table_v, table_s, rowpair, colpair, edge32, sem
):
    def widen(i, c):
        rows = pl.ds(pl.multiple_of(i * 128, 128), 128)
        x32[rows, :] = got_ref[rows, :].astype(F32)
        return c

    lax.fori_loop(0, SEND // 128, widen, 0)
    cells = jnp.concatenate([x32[s * BLK + CAP : s * BLK + CAP + 1, :] for s in range(DEV)], axis=0)
    swapped = pltpu.roll(cells, CAP, axis=1)
    lane = lax.broadcasted_iota(jnp.int32, (DEV, 128), 1)
    first = lane < CAP
    index = jnp.where(
        cells == 0.0, lane, cells.astype(jnp.int32) * TW + swapped.astype(jnp.int32)
    )
    index = jnp.where(first, index, -1)
    repeated = jnp.zeros((DEV, 128), jnp.bool_)
    for d in range(1, GROUP):
        same = (index == pltpu.roll(index, d, axis=1)) & (lane % GROUP >= d)
        repeated = repeated | same
    repeated = jnp.where(first & repeated, 1.0, 0.0).astype(BF16)
    groups = (
        lax.broadcasted_iota(jnp.int32, (128, 128), 0) // GROUP
        == (lax.broadcasted_iota(jnp.int32, (128, 128), 1) - CAP)
    ).astype(F32).astype(BF16)
    flags = jnp.dot(repeated, groups, preferred_element_type=F32).astype(jnp.int32)
    table_v[...] = jnp.where(first, index, flags)
    to_scalar = pltpu.make_async_copy(table_v, table_s, sem)
    to_scalar.start()

    half = DEV // 2
    firsth = lax.broadcasted_iota(jnp.int32, (half, 128), 1) < CAP
    rowpair[...] = jnp.where(firsth, cells[:half], swapped[half:])
    colpair[...] = jnp.where(firsth, swapped[:half], cells[half:])
    col_ids = lax.broadcasted_iota(jnp.int32, (TW, 128), 0).astype(F32)
    row_ids = (lax.broadcasted_iota(jnp.int32, (128, 128), 0) + 1).astype(F32)

    def tally(i, total):
        col_hot = (col_ids == colpair[pl.ds(i, 1), :]).astype(F32).astype(BF16)
        row_hot = (row_ids == rowpair[pl.ds(i, 1), :]).astype(F32).astype(BF16)
        return total + lax.dot_general(
            col_hot, row_hot, (((1,), (1,)), ((), ())), preferred_element_type=F32
        )

    tallies = lax.fori_loop(0, half, tally, jnp.zeros((TW, 128), F32))
    inverse = 1.0 / jnp.maximum(tallies, 1.0)

    def clear(i, c):
        acc[pl.ds(pl.multiple_of(i * 128, 128), 128), :] = jnp.zeros((128, CH), F32)
        return c

    lax.fori_loop(0, (TRASH + TH * TW) // 128, clear, 0)
    to_scalar.wait()

    def source(s, c):
        for g in range(CAP // GROUP):
            clash = table_s[s, CAP + g]

            @pl.when(clash == 0)
            def _():
                index = [table_s[s, g * GROUP + k] for k in range(GROUP)]
                sums = [
                    acc[pl.ds(index[k], 1), :] + x32[pl.ds(s * BLK + g * GROUP + k, 1), :]
                    for k in range(GROUP)
                ]
                for k in range(GROUP):
                    acc[pl.ds(index[k], 1), :] = sums[k]

            @pl.when(clash != 0)
            def _():
                for k in range(GROUP):
                    at = pl.ds(table_s[s, g * GROUP + k], 1)
                    acc[at, :] = acc[at, :] + x32[pl.ds(s * BLK + g * GROUP + k, 1), :]

        return c

    lax.fori_loop(0, DEV, source, 0)
    for i in range(TH):
        scale = jnp.broadcast_to(inverse[:, i : i + 1], (TW, CH))
        mean = acc[TRASH + i * TW : TRASH + (i + 1) * TW, :] * scale
        out_ref[i * TW : (i + 1) * TW, :] = mean.astype(BF16)
        if i == 0:
            top_ref[...] = mean.astype(BF16)
        if i >= TH - 2:
            bottom_ref[(i - TH + 2) * TW : (i - TH + 3) * TW, :] = mean.astype(BF16)
        edge32[0, i : i + 1, :] = mean[0:1]
        edge32[1, i : i + 1, :] = mean[239:240]
        edge32[2, i : i + 1, :] = mean[255:256]
    edge_ref[...] = edge32[...].astype(BF16)


def to_grid(got):
    shapes = [(TH * TW, CH), (TW, CH), (2 * TW, CH), (3, TH, CH)]
    return pl.pallas_call(
        grid_kernel,
        out_shape=[jax.ShapeDtypeStruct(s, BF16) for s in shapes],
        in_specs=[pl.BlockSpec(memory_space=pltpu.VMEM)],
        out_specs=[pl.BlockSpec(memory_space=pltpu.VMEM)] * 4,
        scratch_shapes=[
            pltpu.VMEM((SEND, CH), F32),
            pltpu.VMEM((TRASH + TH * TW, CH), F32),
            pltpu.VMEM((DEV, 128), jnp.int32),
            pltpu.SMEM((DEV, 128), jnp.int32),
            pltpu.VMEM((DEV // 2, 128), F32),
            pltpu.VMEM((DEV // 2, 128), F32),
            pltpu.VMEM((3, TH, CH), F32),
            pltpu.SemaphoreType.DMA,
        ],
        compiler_params=pltpu.CompilerParams(vmem_limit_bytes=40 * 1024 * 1024),
        name="to_grid",
    )(got)


def conv_kernel(
    band_ref, cell_ref, north_ref, south_ref, own_ref, west_ref, east_ref, w1_ref, w2_ref, out_ref,
    field, even, odd, wcol, ecol, hcol,
):
    field[0:2, 1:17] = north_ref[...].reshape(2, 16, 16, CH)
    field[2 + TH, 1:17] = south_ref[...].reshape(16, 16, CH)

    def place(i, c):
        rows = pl.ds(pl.multiple_of(i * TW, TW), TW)
        field[2 + i, 1:17] = cell_ref[rows, :].reshape(16, 16, CH)
        return c

    lax.fori_loop(0, TH, place, 0)
    wcol[...] = west_ref[1].astype(F32)
    ecol[...] = east_ref[...].astype(F32)
    sub = lax.broadcasted_iota(jnp.int32, (16, CH), 0)

    def wrap(r, c):
        before = pltpu.roll(field[r, 16].astype(F32), 1, axis=0)
        field[r, 0] = jnp.where(sub == 0, wcol[pl.ds(r, 1), :], before).astype(BF16)
        after = pltpu.roll(field[r, 1].astype(F32), 15, axis=0)
        field[r, 17] = jnp.where(sub == 15, ecol[pl.ds(r, 1), :], after).astype(BF16)
        return c

    lax.fori_loop(0, TH + 3, wrap, 0)

    taps = [west_ref[0].astype(F32), west_ref[1].astype(F32), own_ref[...].astype(F32)]
    lhs = jnp.concatenate([taps[b][a : a + 40] for a in range(3) for b in range(3)], axis=1)
    hcol[...] = gelu(jnp.dot(lhs.astype(BF16), w1_ref[...], preferred_element_type=F32))
    sub2 = lax.broadcasted_iota(jnp.int32, (16, HID), 0)

    def first(step, c):
        lhs = jnp.concatenate(
            [
                jnp.concatenate(
                    [
                        field[3 * step + r + a, b : b + 16].reshape(TW, CH)
                        for a in range(3)
                        for b in range(3)
                    ],
                    axis=1,
                )
                for r in range(3)
            ],
            axis=0,
        )
        y = gelu(jnp.dot(lhs, w1_ref[...], preferred_element_type=F32))
        y16 = y.astype(BF16).reshape(3, 8, 2, 16, HID)
        for r in range(3):
            hr = 3 * step + r
            odd[hr] = y16[r, :, 0]
            even[hr, 1:9] = y16[r, :, 1]
            before = pltpu.roll(y[r * TW + 240 : r * TW + 256], 1, axis=0)
            even[hr, 0] = jnp.where(sub2 == 0, hcol[pl.ds(hr, 1), :], before).astype(BF16)
        return c

    lax.fori_loop(0, 11, first, 0)

    @pl.when(band_ref[0] == 0)
    def _():
        even[0] = jnp.zeros((9, 16, HID), BF16)
        odd[0] = jnp.zeros((8, 16, HID), BF16)

    out_row = lax.broadcasted_iota(jnp.int32, (128, 128), 0)
    out_col = lax.broadcasted_iota(jnp.int32, (128, 128), 1)
    order = ((out_row % 8) * 16 + out_row // 8 == out_col).astype(F32).astype(BF16)

    def second(step, c):
        lhs = jnp.concatenate(
            [
                jnp.concatenate(
                    [
                        x.reshape(128, HID)
                        for a in range(3)
                        for x in (
                            even[4 * step + 2 * r + a, 0:8],
                            odd[4 * step + 2 * r + a],
                            even[4 * step + 2 * r + a, 1:9],
                        )
                    ],
                    axis=1,
                )
                for r in range(2)
            ],
            axis=0,
        )
        y = gelu(jnp.dot(lhs, w2_ref[...], preferred_element_type=F32)).astype(BF16)
        for r in range(2):
            out_ref[2 * step + r] = jnp.dot(
                order, y[r * 128 : (r + 1) * 128], preferred_element_type=F32
            ).astype(BF16)
        return c

    lax.fori_loop(0, TH // 4, second, 0)


def convolve(band, cells, north, south, own, west, east, w1, w2):
    return pl.pallas_call(
        conv_kernel,
        out_shape=jax.ShapeDtypeStruct((TH // 2, TW // 2, HID), BF16),
        in_specs=[pl.BlockSpec(memory_space=pltpu.SMEM)] + [pl.BlockSpec(memory_space=pltpu.VMEM)] * 8,
        out_specs=pl.BlockSpec(memory_space=pltpu.VMEM),
        scratch_shapes=[
            pltpu.VMEM((TH + 3, 18, 16, CH), BF16),
            pltpu.VMEM((TH + 1, 9, 16, HID), BF16),
            pltpu.VMEM((TH + 1, 8, 16, HID), BF16),
            pltpu.VMEM((COLS, CH), F32),
            pltpu.VMEM((COLS, CH), F32),
            pltpu.VMEM((40, HID), F32),
        ],
        compiler_params=pltpu.CompilerParams(vmem_limit_bytes=48 * 1024 * 1024),
        name="convolve",
    )(band, cells, north, south, own, west, east, w1, w2)


def body(obs_values, obs_dest, obs_cell, obs_count, conv_in, conv_down):
    lat = lax.axis_size("lat")
    lon = lax.axis_size("lon")
    send = pack(obs_values, obs_dest, obs_cell, obs_count)
    got = lax.all_to_all(
        send.reshape(DEV, BLK, CH), ("lat", "lon"), split_axis=0, concat_axis=0, tiled=True
    )
    cells, top, bottom, edge = to_grid(got.reshape(SEND, CH))
    north = lax.ppermute(bottom, "lat", [(i, i + 1) for i in range(lat - 1)])
    south = lax.ppermute(top, "lat", [(i + 1, i) for i in range(lat - 1)])
    north3 = north.reshape(2, TW, CH)
    full = jnp.stack(
        [
            jnp.concatenate(
                [north3[:, at], edge[e], south[at : at + 1], jnp.zeros((COLS - TH - 3, CH), BF16)]
            )
            for e, at in enumerate((0, 239, 255))
        ]
    )
    own = full[0]
    west = lax.ppermute(full[1:], "lon", [(i, (i + 1) % lon) for i in range(lon)])
    east = lax.ppermute(own, "lon", [((i + 1) % lon, i) for i in range(lon)])
    band = lax.axis_index("lat").astype(jnp.int32).reshape(1)
    return convolve(
        band, cells, north, south, own, west, east,
        conv_in.reshape(9 * CH, HID), conv_down.reshape(9 * HID, HID),
    )


def solution(mesh):
    placed = (
        P(("lat", "lon"), None),
        P(("lat", "lon"), None),
        P(("lat", "lon")),
        P(("lat", "lon")),
        P(),
        P(),
    )
    return jax.shard_map(
        body, mesh=mesh, in_specs=placed, out_specs=P("lat", "lon", None), check_vma=False
    )
```

```python
import functools

import jax
import jax.numpy as jnp
from jax import lax
from jax.experimental import pallas as pl
from jax.experimental.pallas import tpu as pltpu
from jax.sharding import PartitionSpec as P

TH = 32
TW = 256
CH = 128
HID = 256
DEV = 128
CAP = 64
ROWS = 4096
BLK = 72
SEND = DEV * BLK
TRASH = 256
GROUP = 8
PART = 32
COLS = 48
F32 = jnp.float32
BF16 = jnp.bfloat16


def gelu(x):
    inner = x * (0.7978845608028654 + 0.035677408136300125 * (x * x))
    return (0.5 * x) * (1.0 + jnp.tanh(inner))


def pack_kernel(
    count_ref, dest_hbm, cell_hbm, val_hbm, out_hbm,
    dest_ref, cell_ref, val_ref, o16, x32, o32, slot_v, slot_s, sem, sem_in, sem_out,
):
    fetches = [
        pltpu.make_async_copy(src, dst, sem_in.at[i])
        for i, (src, dst) in enumerate(((dest_hbm, dest_ref), (cell_hbm, cell_ref), (val_hbm, val_ref)))
    ]
    for fetch in fetches:
        fetch.start()
    count = count_ref[0]
    lane = lax.broadcasted_iota(jnp.int32, (1, 256), 1)
    dest_ids = lax.broadcasted_iota(jnp.int32, (DEV, 256), 0)
    pos_ids = lax.broadcasted_iota(jnp.int32, (CAP, 256), 0)
    upper = (
        lax.broadcasted_iota(jnp.int32, (256, 256), 0)
        < lax.broadcasted_iota(jnp.int32, (256, 256), 1)
    ).astype(F32).astype(BF16)
    fetches[0].wait()
    fetches[1].wait()
    carry = jnp.zeros((DEV, 1), F32)
    cells = jnp.zeros((DEV, 2 * CAP), F32)
    for a in range(ROWS // 256):
        dest = jnp.concatenate([dest_ref[2 * a : 2 * a + 1], dest_ref[2 * a + 1 : 2 * a + 2]], axis=1)
        cell = jnp.concatenate([cell_ref[2 * a : 2 * a + 1], cell_ref[2 * a + 1 : 2 * a + 2]], axis=1)
        live = (lane + 256 * a) < count
        dest_or = jnp.where(live, dest, DEV)
        hot = (dest_ids == dest_or).astype(F32)
        hot16 = hot.astype(BF16)
        before = jnp.dot(hot16, upper, preferred_element_type=F32) + carry
        carry = carry + jnp.sum(hot, axis=1, keepdims=True)
        pos = jnp.sum(hot * before, axis=0, keepdims=True).astype(jnp.int32)
        slot = jnp.where(live, dest * BLK + pos, SEND)
        slot_v[2 * a : 2 * a + 1] = slot[:, :128]
        slot_v[2 * a + 1 : 2 * a + 2] = slot[:, 128:]
        high = (cell // TW + 1).astype(F32)
        low = ((cell % 16) * 16 + (cell % TW) // 16).astype(F32)
        pos_hot = pos_ids == pos
        coded = jnp.concatenate(
            [jnp.where(pos_hot, high, 0.0), jnp.where(pos_hot, low, 0.0)], axis=0
        ).astype(BF16)
        cells = cells + lax.dot_general(
            hot16, coded, (((1,), (1,)), ((), ())), preferred_element_type=F32
        )
    to_scalar = pltpu.make_async_copy(slot_v, slot_s, sem)
    to_scalar.start()
    fetches[2].wait()

    def widen(i, c):
        rows = pl.ds(pl.multiple_of(i * 128, 128), 128)
        x32[rows, :] = val_ref[rows, :].astype(F32)
        return c

    lax.fori_loop(0, ROWS // 128, widen, 0)
    to_scalar.wait()

    def move(i, c):
        base = pl.multiple_of(i * 128, 128)
        for k in range(128):
            o32[pl.ds(slot_s[i, k], 1), :] = x32[pl.ds(base + k, 1), :]
        return c

    lax.fori_loop(0, ROWS // 128, move, 0)
    for d in range(DEV):
        o32[d * BLK + CAP : d * BLK + CAP + 1, :] = cells[d : d + 1, :]

    def narrow(i, c):
        rows = pl.ds(pl.multiple_of(i * 128, 128), 128)
        o16[rows, :] = o32[rows, :].astype(BF16)
        return c

    parts = 4
    stores = []
    for p in range(parts):
        lax.fori_loop(p * SEND // 128 // parts, (p + 1) * SEND // 128 // parts, narrow, 0)
        rows = pl.ds(p * SEND // parts, SEND // parts)
        store = pltpu.make_async_copy(o16.at[rows], out_hbm.at[rows], sem_out.at[p])
        store.start()
        stores.append(store)
    for store in stores:
        store.wait()


def pack(obs_values, obs_dest, obs_cell, obs_count):
    return pl.pallas_call(
        pack_kernel,
        out_shape=jax.ShapeDtypeStruct((SEND, CH), BF16),
        in_specs=[pl.BlockSpec(memory_space=pltpu.SMEM)] + [pl.BlockSpec(memory_space=pl.ANY)] * 3,
        out_specs=pl.BlockSpec(memory_space=pl.ANY),
        scratch_shapes=[
            pltpu.VMEM((32, 128), jnp.int32),
            pltpu.VMEM((32, 128), jnp.int32),
            pltpu.VMEM((ROWS, CH), BF16),
            pltpu.VMEM((SEND, CH), BF16),
            pltpu.VMEM((ROWS, CH), F32),
            pltpu.VMEM((SEND + 8, CH), F32),
            pltpu.VMEM((32, 128), jnp.int32),
            pltpu.SMEM((32, 128), jnp.int32),
            pltpu.SemaphoreType.DMA,
            pltpu.SemaphoreType.DMA((3,)),
            pltpu.SemaphoreType.DMA((4,)),
        ],
        compiler_params=pltpu.CompilerParams(vmem_limit_bytes=60 * 1024 * 1024),
        name="pack",
    )(obs_count, obs_dest.reshape(32, 128), obs_cell.reshape(32, 128), obs_values)


def grid_kernel(
    got_ref, out_ref, top_ref, bottom_ref, edge_ref, x32, acc, acc2, table_v, table_s, rowpair, colpair, edge32, sem
):
    def widen(i, c):
        rows = pl.ds(pl.multiple_of(i * 128, 128), 128)
        x32[rows, :] = got_ref[rows, :].astype(F32)
        return c

    lax.fori_loop(0, SEND // 128, widen, 0)
    cells = jnp.concatenate([x32[s * BLK + CAP : s * BLK + CAP + 1, :] for s in range(DEV)], axis=0)
    swapped = pltpu.roll(cells, CAP, axis=1)
    lane = lax.broadcasted_iota(jnp.int32, (DEV, 128), 1)
    first = lane < CAP
    index = jnp.where(
        cells == 0.0, lane, cells.astype(jnp.int32) * TW + swapped.astype(jnp.int32)
    )
    index = jnp.where(first, index, -1)
    repeated = jnp.zeros((DEV, 128), jnp.bool_)
    for d in range(1, GROUP):
        same = (index == pltpu.roll(index, d, axis=1)) & (lane % GROUP >= d)
        repeated = repeated | same
    repeated = jnp.where(first & repeated, 1.0, 0.0).astype(BF16)
    groups = (
        lax.broadcasted_iota(jnp.int32, (128, 128), 0) // PART
        == (lax.broadcasted_iota(jnp.int32, (128, 128), 1) - CAP)
    ).astype(F32).astype(BF16)
    flags = jnp.dot(repeated, groups, preferred_element_type=F32)
    flags = (flags + pltpu.roll(flags, DEV // 2, axis=0)).astype(jnp.int32)
    table_v[...] = jnp.where(first, index, flags)
    to_scalar = pltpu.make_async_copy(table_v, table_s, sem)
    to_scalar.start()

    half = DEV // 2
    firsth = lax.broadcasted_iota(jnp.int32, (half, 128), 1) < CAP
    rowpair[...] = jnp.where(firsth, cells[:half], swapped[half:])
    colpair[...] = jnp.where(firsth, swapped[:half], cells[half:])
    batch = 8
    col_ids = lax.broadcasted_iota(jnp.int32, (TW, 128), 0).astype(F32)
    row_ids = (lax.broadcasted_iota(jnp.int32, (128, 128), 0) + 1).astype(F32)

    def tally(i, total):
        at = [pl.ds(i * batch + k, 1) for k in range(batch)]
        col_hot = jnp.concatenate(
            [(col_ids == colpair[r, :]).astype(F32).astype(BF16) for r in at], axis=1
        )
        row_hot = jnp.concatenate(
            [(row_ids == rowpair[r, :]).astype(F32).astype(BF16) for r in at], axis=1
        )
        return total + lax.dot_general(
            col_hot, row_hot, (((1,), (1,)), ((), ())), preferred_element_type=F32
        )

    tallies = lax.fori_loop(0, half // batch, tally, jnp.zeros((TW, 128), F32))
    inverse = 1.0 / jnp.maximum(tallies, 1.0)

    def clear(i, c):
        acc[pl.ds(pl.multiple_of(i * 128, 128), 128), :] = jnp.zeros((128, CH), F32)
        acc2[pl.ds(pl.multiple_of(i * 128, 128), 128), :] = jnp.zeros((128, CH), F32)
        return c

    lax.fori_loop(0, (TRASH + TH * TW) // 128, clear, 0)
    to_scalar.wait()

    def source(s, c):
        pairs = ((acc, s), (acc2, s + half))
        for p in range(CAP // PART):
            clash = table_s[s, CAP + p]

            @pl.when(clash == 0)
            def _():
                for g in range(p * PART // GROUP, (p + 1) * PART // GROUP):
                    slots = range(g * GROUP, (g + 1) * GROUP)
                    index = [[pl.ds(table_s[t, k], 1) for k in slots] for _, t in pairs]
                    sums = [
                        [a[at, :] + x32[pl.ds(t * BLK + k, 1), :] for at, k in zip(ix, slots)]
                        for (a, t), ix in zip(pairs, index)
                    ]
                    for (a, _), ix, new in zip(pairs, index, sums):
                        for at, value in zip(ix, new):
                            a[at, :] = value

            @pl.when(clash != 0)
            def _():
                for k in range(p * PART, (p + 1) * PART):
                    for a, t in pairs:
                        at = pl.ds(table_s[t, k], 1)
                        a[at, :] = a[at, :] + x32[pl.ds(t * BLK + k, 1), :]

        return c

    lax.fori_loop(0, half, source, 0)
    for i in range(TH):
        scale = jnp.broadcast_to(inverse[:, i : i + 1], (TW, CH))
        rows = slice(TRASH + i * TW, TRASH + (i + 1) * TW)
        mean = (acc[rows, :] + acc2[rows, :]) * scale
        out_ref[i * TW : (i + 1) * TW, :] = mean.astype(BF16)
        if i == 0:
            top_ref[...] = mean.astype(BF16)
        if i >= TH - 2:
            bottom_ref[(i - TH + 2) * TW : (i - TH + 3) * TW, :] = mean.astype(BF16)
        edge32[0, i : i + 1, :] = mean[0:1]
        edge32[1, i : i + 1, :] = mean[239:240]
        edge32[2, i : i + 1, :] = mean[255:256]
    edge_ref[...] = edge32[...].astype(BF16)


def to_grid(got):
    shapes = [(TH * TW, CH), (TW, CH), (2 * TW, CH), (3, TH, CH)]
    return pl.pallas_call(
        grid_kernel,
        out_shape=[jax.ShapeDtypeStruct(s, BF16) for s in shapes],
        in_specs=[pl.BlockSpec(memory_space=pltpu.VMEM)],
        out_specs=[pl.BlockSpec(memory_space=pltpu.VMEM)] * 4,
        scratch_shapes=[
            pltpu.VMEM((SEND, CH), F32),
            pltpu.VMEM((TRASH + TH * TW, CH), F32),
            pltpu.VMEM((TRASH + TH * TW, CH), F32),
            pltpu.VMEM((DEV, 128), jnp.int32),
            pltpu.SMEM((DEV, 128), jnp.int32),
            pltpu.VMEM((DEV // 2, 128), F32),
            pltpu.VMEM((DEV // 2, 128), F32),
            pltpu.VMEM((3, TH, CH), F32),
            pltpu.SemaphoreType.DMA,
        ],
        compiler_params=pltpu.CompilerParams(vmem_limit_bytes=24 * 1024 * 1024),
        name="to_grid",
    )(got)


def conv_kernel(
    band_ref, cell_ref, north_ref, south_ref, own_ref, west_ref, east_ref, w1_ref, w2_ref, out_ref,
    field, even, odd, wcol, ecol, hcol,
):
    field[0:2, 1:17] = north_ref[...].reshape(2, 16, 16, CH)
    field[2 + TH, 1:17] = south_ref[...].reshape(16, 16, CH)

    def place(i, c):
        rows = pl.ds(pl.multiple_of(i * TW, TW), TW)
        field[2 + i, 1:17] = cell_ref[rows, :].reshape(16, 16, CH)
        return c

    lax.fori_loop(0, TH, place, 0)
    wcol[...] = west_ref[1].astype(F32)
    ecol[...] = east_ref[...].astype(F32)
    sub = lax.broadcasted_iota(jnp.int32, (16, CH), 0)

    def wrap(r, c):
        before = pltpu.roll(field[r, 16].astype(F32), 1, axis=0)
        field[r, 0] = jnp.where(sub == 0, wcol[pl.ds(r, 1), :], before).astype(BF16)
        after = pltpu.roll(field[r, 1].astype(F32), 15, axis=0)
        field[r, 17] = jnp.where(sub == 15, ecol[pl.ds(r, 1), :], after).astype(BF16)
        return c

    lax.fori_loop(0, TH + 3, wrap, 0)

    taps = [west_ref[0].astype(F32), west_ref[1].astype(F32), own_ref[...].astype(F32)]
    lhs = jnp.concatenate([taps[b][a : a + 40] for a in range(3) for b in range(3)], axis=1)
    hcol[...] = gelu(jnp.dot(lhs.astype(BF16), w1_ref[...], preferred_element_type=F32))
    sub2 = lax.broadcasted_iota(jnp.int32, (16, HID), 0)

    def first(step, c):
        lhs = jnp.concatenate(
            [
                jnp.concatenate(
                    [
                        field[3 * step + r + a, b : b + 16].reshape(TW, CH)
                        for a in range(3)
                        for b in range(3)
                    ],
                    axis=1,
                )
                for r in range(3)
            ],
            axis=0,
        )
        y = gelu(jnp.dot(lhs, w1_ref[...], preferred_element_type=F32))
        y16 = y.astype(BF16).reshape(3, 8, 2, 16, HID)
        for r in range(3):
            hr = 3 * step + r
            odd[hr] = y16[r, :, 0]
            even[hr, 1:9] = y16[r, :, 1]
            before = pltpu.roll(y[r * TW + 240 : r * TW + 256], 1, axis=0)
            even[hr, 0] = jnp.where(sub2 == 0, hcol[pl.ds(hr, 1), :], before).astype(BF16)
        return c

    lax.fori_loop(0, 11, first, 0)

    @pl.when(band_ref[0] == 0)
    def _():
        even[0] = jnp.zeros((9, 16, HID), BF16)
        odd[0] = jnp.zeros((8, 16, HID), BF16)

    out_row = lax.broadcasted_iota(jnp.int32, (128, 128), 0)
    out_col = lax.broadcasted_iota(jnp.int32, (128, 128), 1)
    order = ((out_row % 8) * 16 + out_row // 8 == out_col).astype(F32).astype(BF16)

    def second(step, c):
        lhs = jnp.concatenate(
            [
                jnp.concatenate(
                    [
                        x.reshape(128, HID)
                        for a in range(3)
                        for x in (
                            even[4 * step + 2 * r + a, 0:8],
                            odd[4 * step + 2 * r + a],
                            even[4 * step + 2 * r + a, 1:9],
                        )
                    ],
                    axis=1,
                )
                for r in range(2)
            ],
            axis=0,
        )
        y = gelu(jnp.dot(lhs, w2_ref[...], preferred_element_type=F32)).astype(BF16)
        for r in range(2):
            out_ref[2 * step + r] = jnp.dot(
                order, y[r * 128 : (r + 1) * 128], preferred_element_type=F32
            ).astype(BF16)
        return c

    lax.fori_loop(0, TH // 4, second, 0)


def convolve(band, cells, north, south, own, west, east, w1, w2):
    return pl.pallas_call(
        conv_kernel,
        out_shape=jax.ShapeDtypeStruct((TH // 2, TW // 2, HID), BF16),
        in_specs=[pl.BlockSpec(memory_space=pltpu.SMEM)] + [pl.BlockSpec(memory_space=pltpu.VMEM)] * 8,
        out_specs=pl.BlockSpec(memory_space=pltpu.VMEM),
        scratch_shapes=[
            pltpu.VMEM((TH + 3, 18, 16, CH), BF16),
            pltpu.VMEM((TH + 1, 9, 16, HID), BF16),
            pltpu.VMEM((TH + 1, 8, 16, HID), BF16),
            pltpu.VMEM((COLS, CH), F32),
            pltpu.VMEM((COLS, CH), F32),
            pltpu.VMEM((40, HID), F32),
        ],
        compiler_params=pltpu.CompilerParams(vmem_limit_bytes=24 * 1024 * 1024),
        name="convolve",
    )(band, cells, north, south, own, west, east, w1, w2)


def body(obs_values, obs_dest, obs_cell, obs_count, conv_in, conv_down):
    lat = lax.axis_size("lat")
    lon = lax.axis_size("lon")
    send = pack(obs_values, obs_dest, obs_cell, obs_count)
    got = lax.all_to_all(
        send.reshape(DEV, BLK, CH), ("lat", "lon"), split_axis=0, concat_axis=0, tiled=True
    )
    cells, top, bottom, edge = to_grid(got.reshape(SEND, CH))
    north = lax.ppermute(bottom, "lat", [(i, i + 1) for i in range(lat - 1)])
    south = lax.ppermute(top, "lat", [(i + 1, i) for i in range(lat - 1)])
    north3 = north.reshape(2, TW, CH)
    full = jnp.stack(
        [
            jnp.concatenate(
                [north3[:, at], edge[e], south[at : at + 1], jnp.zeros((COLS - TH - 3, CH), BF16)]
            )
            for e, at in enumerate((0, 239, 255))
        ]
    )
    own = full[0]
    west = lax.ppermute(full[1:], "lon", [(i, (i + 1) % lon) for i in range(lon)])
    east = lax.ppermute(own, "lon", [((i + 1) % lon, i) for i in range(lon)])
    band = lax.axis_index("lat").astype(jnp.int32).reshape(1)
    return convolve(
        band, cells, north, south, own, west, east,
        conv_in.reshape(9 * CH, HID), conv_down.reshape(9 * HID, HID),
    )


def solution(mesh):
    placed = (
        P(("lat", "lon"), None),
        P(("lat", "lon"), None),
        P(("lat", "lon")),
        P(("lat", "lon")),
        P(),
        P(),
    )
    return jax.shard_map(
        body, mesh=mesh, in_specs=placed, out_specs=P("lat", "lon", None), check_vma=False
    )
```

```python
import functools

import jax
import jax.numpy as jnp
from jax import lax
from jax.experimental import pallas as pl
from jax.experimental.pallas import tpu as pltpu
from jax.sharding import PartitionSpec as P

TH = 32
TW = 256
CH = 128
HID = 256
DEV = 128
CAP = 64
ROWS = 4096
BLK = 66
SEND = DEV * BLK
TRASH = 256
GROUP = 8
PART = 32
FIRST = 11
SECOND = 8
COLS = 48
F32 = jnp.float32
BF16 = jnp.bfloat16


def gelu(x):
    inner = x * (0.7978845608028654 + 0.035677408136300125 * (x * x))
    return (0.5 * x) * (1.0 + jnp.tanh(inner))


def pack_kernel(
    count_ref, dest_hbm, cell_hbm, val_hbm, out_hbm,
    dest_ref, cell_ref, val_ref, o16, x32, o32, slot_v, slot_s, sem, sem_in, sem_out,
):
    fetches = [
        pltpu.make_async_copy(src, dst, sem_in.at[i])
        for i, (src, dst) in enumerate(((dest_hbm, dest_ref), (cell_hbm, cell_ref), (val_hbm, val_ref)))
    ]
    for fetch in fetches:
        fetch.start()
    count = count_ref[0]
    lane = lax.broadcasted_iota(jnp.int32, (1, 256), 1)
    dest_ids = lax.broadcasted_iota(jnp.int32, (DEV, 256), 0)
    pos_ids = lax.broadcasted_iota(jnp.int32, (CAP, 256), 0)
    upper = (
        lax.broadcasted_iota(jnp.int32, (256, 256), 0)
        < lax.broadcasted_iota(jnp.int32, (256, 256), 1)
    ).astype(F32).astype(BF16)
    fetches[0].wait()
    fetches[1].wait()
    carry = jnp.zeros((DEV, 1), F32)
    cells = jnp.zeros((DEV, 2 * CAP), F32)
    slots = []
    for a in range(ROWS // 256):
        dest = jnp.concatenate([dest_ref[2 * a : 2 * a + 1], dest_ref[2 * a + 1 : 2 * a + 2]], axis=1)
        cell = jnp.concatenate([cell_ref[2 * a : 2 * a + 1], cell_ref[2 * a + 1 : 2 * a + 2]], axis=1)
        live = (lane + 256 * a) < count
        dest_or = jnp.where(live, dest, DEV)
        hot = (dest_ids == dest_or).astype(F32)
        hot16 = hot.astype(BF16)
        before = jnp.dot(hot16, upper, preferred_element_type=F32) + carry
        carry = carry + jnp.sum(hot, axis=1, keepdims=True)
        pos = jnp.sum(hot * before, axis=0, keepdims=True).astype(jnp.int32)
        slot = jnp.where(live, dest * BLK + pos, SEND)
        slots += [slot[:, :128], slot[:, 128:]]
        high = (cell // TW + 1).astype(F32)
        low = ((cell % 16) * 16 + (cell % TW) // 16).astype(F32)
        pos_hot = pos_ids == pos
        coded = jnp.concatenate(
            [jnp.where(pos_hot, high, 0.0), jnp.where(pos_hot, low, 0.0)], axis=0
        ).astype(BF16)
        cells = cells + lax.dot_general(
            hot16, coded, (((1,), (1,)), ((), ())), preferred_element_type=F32
        )
    slots = jnp.concatenate(slots + [jnp.zeros((96, 128), jnp.int32)], axis=0)
    slot_v[...] = slots.T
    to_scalar = pltpu.make_async_copy(slot_v, slot_s, sem)
    to_scalar.start()
    fetches[2].wait()

    def widen(i, c):
        rows = pl.ds(pl.multiple_of(i * 128, 128), 128)
        x32[rows, :] = val_ref[rows, :].astype(F32)
        return c

    lax.fori_loop(0, ROWS // 128, widen, 0)
    to_scalar.wait()

    def move(i, c):
        base = pl.multiple_of(i * 128, 128)
        for k in range(128):
            o32[pl.ds(slot_s.at[k][i], 1), :] = x32[pl.ds(base + k, 1), :]
        return c

    lax.fori_loop(0, ROWS // 128, move, 0)
    for d in range(DEV):
        o32[d * BLK + CAP : d * BLK + CAP + 1, :] = cells[d : d + 1, :]

    def narrow(i, c):
        rows = pl.ds(pl.multiple_of(i * 128, 128), 128)
        o16[rows, :] = o32[rows, :].astype(BF16)
        return c

    parts = 3
    stores = []
    for p in range(parts):
        lax.fori_loop(p * SEND // 128 // parts, (p + 1) * SEND // 128 // parts, narrow, 0)
        rows = pl.ds(p * SEND // parts, SEND // parts)
        store = pltpu.make_async_copy(o16.at[rows], out_hbm.at[rows], sem_out.at[p])
        store.start()
        stores.append(store)
    for store in stores:
        store.wait()


def pack(obs_values, obs_dest, obs_cell, obs_count):
    return pl.pallas_call(
        pack_kernel,
        out_shape=jax.ShapeDtypeStruct((SEND, CH), BF16),
        in_specs=[pl.BlockSpec(memory_space=pltpu.SMEM)] + [pl.BlockSpec(memory_space=pl.ANY)] * 3,
        out_specs=pl.BlockSpec(memory_space=pl.ANY),
        scratch_shapes=[
            pltpu.VMEM((32, 128), jnp.int32),
            pltpu.VMEM((32, 128), jnp.int32),
            pltpu.VMEM((ROWS, CH), BF16),
            pltpu.VMEM((SEND, CH), BF16),
            pltpu.VMEM((ROWS, CH), F32),
            pltpu.VMEM((SEND + 8, CH), F32),
            pltpu.VMEM((128, 128), jnp.int32),
            pltpu.SMEM((128, 128), jnp.int32),
            pltpu.SemaphoreType.DMA,
            pltpu.SemaphoreType.DMA((3,)),
            pltpu.SemaphoreType.DMA((3,)),
        ],
        compiler_params=pltpu.CompilerParams(vmem_limit_bytes=60 * 1024 * 1024),
        name="pack",
    )(obs_count, obs_dest.reshape(32, 128), obs_cell.reshape(32, 128), obs_values)


def grid_kernel(
    got_ref, out_hbm, top_ref, bottom_ref, edge_ref,
    out_ref, x32, acc, acc2, table_v, table_s, rowpair, colpair, edge32, sem, sem_out,
):
    parts = 4

    def clear(i, c):
        acc[pl.ds(pl.multiple_of(i * 128, 128), 128), :] = jnp.zeros((128, CH), F32)
        acc2[pl.ds(pl.multiple_of(i * 128, 128), 128), :] = jnp.zeros((128, CH), F32)
        return c

    lax.fori_loop(0, (TRASH + TH * TW) // 128, clear, 0)

    def widen(i, c):
        rows = pl.ds(pl.multiple_of(i * 192, 192), 192)
        x32[rows, :] = got_ref[rows, :].astype(F32)
        return c

    lax.fori_loop(0, SEND // 192, widen, 0)
    cells = jnp.concatenate([x32[s * BLK + CAP : s * BLK + CAP + 1, :] for s in range(DEV)], axis=0)
    swapped = pltpu.roll(cells, CAP, axis=1)
    lane = lax.broadcasted_iota(jnp.int32, (DEV, 128), 1)
    first = lane < CAP
    index = jnp.where(
        cells == 0.0, lane, cells.astype(jnp.int32) * TW + swapped.astype(jnp.int32)
    )
    index = jnp.where(first, index, -1)
    repeated = jnp.zeros((DEV, 128), jnp.bool_)
    for d in range(1, GROUP):
        same = (index == pltpu.roll(index, d, axis=1)) & (lane % GROUP >= d)
        repeated = repeated | same
    repeated = jnp.where(first & repeated, 1.0, 0.0).astype(BF16)
    groups = (
        lax.broadcasted_iota(jnp.int32, (128, 128), 0) // PART
        == (lax.broadcasted_iota(jnp.int32, (128, 128), 1) - CAP)
    ).astype(F32).astype(BF16)
    flags = jnp.dot(repeated, groups, preferred_element_type=F32)
    flags = (flags + pltpu.roll(flags, DEV // 2, axis=0)).astype(jnp.int32)
    table_v[...] = jnp.where(first, index, flags).T
    to_scalar = pltpu.make_async_copy(table_v, table_s, sem)
    to_scalar.start()

    half = DEV // 2
    firsth = lax.broadcasted_iota(jnp.int32, (half, 128), 1) < CAP
    rowpair[...] = jnp.where(firsth, cells[:half], swapped[half:])
    colpair[...] = jnp.where(firsth, swapped[:half], cells[half:])
    batch = 8
    col_ids = lax.broadcasted_iota(jnp.int32, (TW, 128), 0).astype(F32)
    row_ids = (lax.broadcasted_iota(jnp.int32, (128, 128), 0) + 1).astype(F32)

    def tally(i, total):
        at = [pl.ds(i * batch + k, 1) for k in range(batch)]
        col_hot = jnp.concatenate(
            [(col_ids == colpair[r, :]).astype(F32).astype(BF16) for r in at], axis=1
        )
        row_hot = jnp.concatenate(
            [(row_ids == rowpair[r, :]).astype(F32).astype(BF16) for r in at], axis=1
        )
        return total + lax.dot_general(
            col_hot, row_hot, (((1,), (1,)), ((), ())), preferred_element_type=F32
        )

    tallies = lax.fori_loop(0, half // batch, tally, jnp.zeros((TW, 128), F32))
    inverse = 1.0 / jnp.maximum(tallies, 1.0)

    to_scalar.wait()

    def source(s, c):
        pairs = ((acc, s), (acc2, s + half))
        for p in range(CAP // PART):
            clash = table_s.at[CAP + p][s]

            @pl.when(clash == 0)
            def _():
                for g in range(p * PART // GROUP, (p + 1) * PART // GROUP):
                    slots = range(g * GROUP, (g + 1) * GROUP)
                    index = [[pl.ds(table_s.at[k][t], 1) for k in slots] for _, t in pairs]
                    sums = [
                        [a[at, :] + x32[pl.ds(t * BLK + k, 1), :] for at, k in zip(ix, slots)]
                        for (a, t), ix in zip(pairs, index)
                    ]
                    for (a, _), ix, new in zip(pairs, index, sums):
                        for at, value in zip(ix, new):
                            a[at, :] = value

            @pl.when(clash != 0)
            def _():
                for k in range(p * PART, (p + 1) * PART):
                    for a, t in pairs:
                        at = pl.ds(table_s.at[k][t], 1)
                        a[at, :] = a[at, :] + x32[pl.ds(t * BLK + k, 1), :]

        return c

    lax.fori_loop(0, half, source, 0)
    stores = []
    for i in range(TH):
        scale = jnp.broadcast_to(inverse[:, i : i + 1], (TW, CH))
        rows = slice(TRASH + i * TW, TRASH + (i + 1) * TW)
        mean = (acc[rows, :] + acc2[rows, :]) * scale
        out_ref[i * TW : (i + 1) * TW, :] = mean.astype(BF16)
        if i == 0:
            top_ref[...] = mean.astype(BF16)
        if i >= TH - 2:
            bottom_ref[(i - TH + 2) * TW : (i - TH + 3) * TW, :] = mean.astype(BF16)
        edge32[0, i : i + 1, :] = mean[0:1]
        edge32[1, i : i + 1, :] = mean[239:240]
        edge32[2, i : i + 1, :] = mean[255:256]
        if (i + 1) % (TH // parts) == 0:
            p = i // (TH // parts)
            rows = pl.ds(p * (TH // parts) * TW, (TH // parts) * TW)
            store = pltpu.make_async_copy(out_ref.at[rows], out_hbm.at[rows], sem_out.at[p])
            store.start()
            stores.append(store)
    edge_ref[...] = edge32[...].astype(BF16)
    for store in stores:
        store.wait()


def to_grid(got):
    shapes = [(TH * TW, CH), (TW, CH), (2 * TW, CH), (3, TH, CH)]
    return pl.pallas_call(
        grid_kernel,
        out_shape=[jax.ShapeDtypeStruct(s, BF16) for s in shapes],
        in_specs=[pl.BlockSpec(memory_space=pltpu.VMEM)],
        out_specs=[pl.BlockSpec(memory_space=pl.ANY)] + [pl.BlockSpec(memory_space=pltpu.VMEM)] * 3,
        scratch_shapes=[
            pltpu.VMEM((TH * TW, CH), BF16),
            pltpu.VMEM((SEND, CH), F32),
            pltpu.VMEM((TRASH + TH * TW, CH), F32),
            pltpu.VMEM((TRASH + TH * TW, CH), F32),
            pltpu.VMEM((DEV, 128), jnp.int32),
            pltpu.SMEM((DEV, 128), jnp.int32),
            pltpu.VMEM((DEV // 2, 128), F32),
            pltpu.VMEM((DEV // 2, 128), F32),
            pltpu.VMEM((3, TH, CH), F32),
            pltpu.SemaphoreType.DMA,
            pltpu.SemaphoreType.DMA((4,)),
        ],
        compiler_params=pltpu.CompilerParams(vmem_limit_bytes=60 * 1024 * 1024),
        name="to_grid",
    )(got)


def conv_kernel(
    band_ref, cell_hbm, north_hbm, south_hbm, own_hbm, west_hbm, east_hbm, w1_hbm, w2_hbm, out_ref,
    field, even, odd, own_ref, west_ref, east_ref, wcol, ecol, hcol, w1_ref, w2_ref, o32, sem,
):
    pairs = (
        (west_hbm, west_ref),
        (east_hbm, east_ref),
        (own_hbm, own_ref),
        (north_hbm, field.at[pl.ds(0, 2), pl.ds(1, 16)]),
        (south_hbm, field.at[2 + TH, pl.ds(1, 16)]),
        (cell_hbm, field.at[pl.ds(2, TH), pl.ds(1, 16)]),
        (w1_hbm, w1_ref),
        (w2_hbm, w2_ref),
    )
    fetches = [pltpu.make_async_copy(src, dst, sem.at[i]) for i, (src, dst) in enumerate(pairs)]
    for fetch in fetches:
        fetch.start()
    for fetch in fetches[:6]:
        fetch.wait()
    wcol[...] = west_ref[1].astype(F32)
    ecol[...] = east_ref[...].astype(F32)
    sub = lax.broadcasted_iota(jnp.int32, (16, CH), 0)

    def wrap(r, c):
        before = pltpu.roll(field[r, 16].astype(F32), 1, axis=0)
        field[r, 0] = jnp.where(sub == 0, wcol[pl.ds(r, 1), :], before).astype(BF16)
        after = pltpu.roll(field[r, 1].astype(F32), 15, axis=0)
        field[r, 17] = jnp.where(sub == 15, ecol[pl.ds(r, 1), :], after).astype(BF16)
        return c

    lax.fori_loop(0, TH + 3, wrap, 0, unroll=5)
    fetches[6].wait()

    taps = [west_ref[0].astype(F32), west_ref[1].astype(F32), own_ref[...].astype(F32)]
    lhs = jnp.concatenate([taps[b][a : a + 40] for a in range(3) for b in range(3)], axis=1)
    hcol[...] = gelu(jnp.dot(lhs.astype(BF16), w1_ref[...], preferred_element_type=F32))
    sub2 = lax.broadcasted_iota(jnp.int32, (16, HID), 0)

    def first(step, c):
        lhs = jnp.concatenate(
            [
                field[pl.ds(FIRST * step + a, FIRST), b : b + 16].reshape(FIRST * TW, CH)
                for a in range(3)
                for b in range(3)
            ],
            axis=1,
        )
        y = gelu(jnp.dot(lhs, w1_ref[...], preferred_element_type=F32))
        y16 = y.astype(BF16).reshape(FIRST, 8, 2, 16, HID)
        for r in range(FIRST):
            hr = FIRST * step + r
            odd[hr] = y16[r, :, 0]
            even[hr, 1:9] = y16[r, :, 1]
            before = pltpu.roll(y[r * TW + 240 : r * TW + 256], 1, axis=0)
            even[hr, 0] = jnp.where(sub2 == 0, hcol[pl.ds(hr, 1), :], before).astype(BF16)
        return c

    lax.fori_loop(0, (TH + 1) // FIRST, first, 0)

    @pl.when(band_ref[0] == 0)
    def _():
        even[0] = jnp.zeros((9, 16, HID), BF16)
        odd[0] = jnp.zeros((8, 16, HID), BF16)

    fetches[7].wait()

    def second(step, c):
        lhs = jnp.concatenate(
            [
                jnp.concatenate(
                    [
                        x.reshape(128, HID)
                        for a in range(3)
                        for x in (
                            even[2 * (SECOND * step + r) + a, 0:8],
                            odd[2 * (SECOND * step + r) + a],
                            even[2 * (SECOND * step + r) + a, 1:9],
                        )
                    ],
                    axis=1,
                )
                for r in range(SECOND)
            ],
            axis=0,
        )
        y = gelu(jnp.dot(lhs, w2_ref[...], preferred_element_type=F32))
        for r in range(SECOND):
            for h in range(2):
                for t in range(8):
                    o32[r, h, pl.ds(t, 16, stride=8), :] = y[
                        r * 128 + t * 16 : r * 128 + (t + 1) * 16, h * 128 : (h + 1) * 128
                    ]
            out_ref[SECOND * step + r] = jnp.concatenate([o32[r, 0], o32[r, 1]], axis=1).astype(BF16)
        return c

    lax.fori_loop(0, TH // 2 // SECOND, second, 0)


def convolve(band, cells, north, south, own, west, east, w1, w2):
    return pl.pallas_call(
        conv_kernel,
        out_shape=jax.ShapeDtypeStruct((TH // 2, TW // 2, HID), BF16),
        in_specs=[pl.BlockSpec(memory_space=pltpu.SMEM)] + [pl.BlockSpec(memory_space=pl.ANY)] * 8,
        out_specs=pl.BlockSpec(memory_space=pltpu.VMEM),
        scratch_shapes=[
            pltpu.VMEM((TH + 3, 18, 16, CH), BF16),
            pltpu.VMEM((TH + 1, 9, 16, HID), BF16),
            pltpu.VMEM((TH + 1, 8, 16, HID), BF16),
            pltpu.VMEM((COLS, CH), BF16),
            pltpu.VMEM((2, COLS, CH), BF16),
            pltpu.VMEM((COLS, CH), BF16),
            pltpu.VMEM((COLS, CH), F32),
            pltpu.VMEM((COLS, CH), F32),
            pltpu.VMEM((40, HID), F32),
            pltpu.VMEM((9 * CH, HID), BF16),
            pltpu.VMEM((9 * HID, HID), BF16),
            pltpu.VMEM((SECOND, 2, TW // 2, 128), F32),
            pltpu.SemaphoreType.DMA((8,)),
        ],
        compiler_params=pltpu.CompilerParams(vmem_limit_bytes=56 * 1024 * 1024),
        name="convolve",
    )(
        band, cells.reshape(TH, 16, 16, CH), north.reshape(2, 16, 16, CH), south.reshape(16, 16, CH),
        own, west, east, w1, w2,
    )


def body(obs_values, obs_dest, obs_cell, obs_count, conv_in, conv_down):
    lat = lax.axis_size("lat")
    lon = lax.axis_size("lon")
    send = pack(obs_values, obs_dest, obs_cell, obs_count)
    got = lax.all_to_all(
        send.reshape(DEV, BLK // 2, 2, CH), ("lat", "lon"), split_axis=0, concat_axis=0, tiled=True
    )
    cells, top, bottom, edge = to_grid(got.reshape(SEND, CH))
    north = lax.ppermute(bottom, "lat", [(i, i + 1) for i in range(lat - 1)])
    south = lax.ppermute(top, "lat", [(i + 1, i) for i in range(lat - 1)])
    north3 = north.reshape(2, TW, CH)
    full = jnp.stack(
        [
            jnp.concatenate(
                [north3[:, at], edge[e], south[at : at + 1], jnp.zeros((COLS - TH - 3, CH), BF16)]
            )
            for e, at in enumerate((0, 239, 255))
        ]
    )
    own = full[0]
    west = lax.ppermute(full[1:], "lon", [(i, (i + 1) % lon) for i in range(lon)])
    east = lax.ppermute(own, "lon", [((i + 1) % lon, i) for i in range(lon)])
    band = lax.axis_index("lat").astype(jnp.int32).reshape(1)
    return convolve(
        band, cells, north, south, own, west, east,
        conv_in.reshape(9 * CH, HID), conv_down.reshape(9 * HID, HID),
    )


def solution(mesh):
    placed = (
        P(("lat", "lon"), None),
        P(("lat", "lon"), None),
        P(("lat", "lon")),
        P(("lat", "lon")),
        P(),
        P(),
    )
    return jax.shard_map(
        body, mesh=mesh, in_specs=placed, out_specs=P("lat", "lon", None), check_vma=False
    )
```

```python
import functools

import jax
import jax.numpy as jnp
from jax import lax
from jax.experimental import pallas as pl
from jax.experimental.pallas import tpu as pltpu
from jax.sharding import PartitionSpec as P

TH = 32
TW = 256
CH = 128
HID = 256
DEV = 128
CAP = 64
ROWS = 4096
BLK = 66
SEND = DEV * BLK
TRASH = 256
GROUP = 8
PART = 32
FIRST = 11
SECOND = 8
COLS = 48
F32 = jnp.float32
BF16 = jnp.bfloat16


def gelu(x):
    inner = x * (0.7978845608028654 + 0.035677408136300125 * (x * x))
    return (0.5 * x) * (1.0 + jnp.tanh(inner))


def pack_kernel(
    count_ref, dest_hbm, cell_hbm, val_hbm, out_hbm,
    dest_ref, cell_ref, val_ref, o16, x32, o32, slot_v, slot_s, sem, sem_in, sem_out,
):
    fetches = [
        pltpu.make_async_copy(src, dst, sem_in.at[i])
        for i, (src, dst) in enumerate(((dest_hbm, dest_ref), (cell_hbm, cell_ref), (val_hbm, val_ref)))
    ]
    for fetch in fetches:
        fetch.start()
    count = count_ref[0]
    lane = lax.broadcasted_iota(jnp.int32, (1, 256), 1)
    dest_ids = lax.broadcasted_iota(jnp.int32, (DEV, 256), 0)
    pos_ids = lax.broadcasted_iota(jnp.int32, (CAP, 256), 0)
    upper = (
        lax.broadcasted_iota(jnp.int32, (256, 256), 0)
        < lax.broadcasted_iota(jnp.int32, (256, 256), 1)
    ).astype(F32).astype(BF16)
    fetches[0].wait()
    fetches[1].wait()
    carry = jnp.zeros((DEV, 1), F32)
    cells = jnp.zeros((DEV, 2 * CAP), F32)
    slots = []
    for a in range(ROWS // 256):
        dest = jnp.concatenate([dest_ref[2 * a : 2 * a + 1], dest_ref[2 * a + 1 : 2 * a + 2]], axis=1)
        cell = jnp.concatenate([cell_ref[2 * a : 2 * a + 1], cell_ref[2 * a + 1 : 2 * a + 2]], axis=1)
        live = (lane + 256 * a) < count
        dest_or = jnp.where(live, dest, DEV)
        hot = (dest_ids == dest_or).astype(F32)
        hot16 = hot.astype(BF16)
        before = jnp.dot(hot16, upper, preferred_element_type=F32) + carry
        carry = carry + jnp.sum(hot, axis=1, keepdims=True)
        pos = jnp.sum(hot * before, axis=0, keepdims=True).astype(jnp.int32)
        slot = jnp.where(live, dest * BLK + pos, SEND)
        slots += [slot[:, :128], slot[:, 128:]]
        high = (cell // TW + 1).astype(F32)
        low = ((cell % 16) * 16 + (cell % TW) // 16).astype(F32)
        pos_hot = pos_ids == pos
        coded = jnp.concatenate(
            [jnp.where(pos_hot, high, 0.0), jnp.where(pos_hot, low, 0.0)], axis=0
        ).astype(BF16)
        cells = cells + lax.dot_general(
            hot16, coded, (((1,), (1,)), ((), ())), preferred_element_type=F32
        )
    slots = jnp.concatenate(slots + [jnp.zeros((96, 128), jnp.int32)], axis=0)
    slot_v[...] = slots.T
    to_scalar = pltpu.make_async_copy(slot_v, slot_s, sem)
    to_scalar.start()
    fetches[2].wait()

    def widen(i, c):
        rows = pl.ds(pl.multiple_of(i * 128, 128), 128)
        x32[rows, :] = val_ref[rows, :].astype(F32)
        return c

    lax.fori_loop(0, ROWS // 128, widen, 0)
    to_scalar.wait()

    def move(i, c):
        base = pl.multiple_of(i * 128, 128)
        for k in range(128):
            o32[pl.ds(slot_s.at[k][i], 1), :] = x32[pl.ds(base + k, 1), :]
        return c

    lax.fori_loop(0, ROWS // 128, move, 0)
    for d in range(DEV):
        o32[d * BLK + CAP : d * BLK + CAP + 1, :] = cells[d : d + 1, :]

    def narrow(i, c):
        rows = pl.ds(pl.multiple_of(i * 128, 128), 128)
        o16[rows, :] = o32[rows, :].astype(BF16)
        return c

    parts = 3
    stores = []
    for p in range(parts):
        lax.fori_loop(p * SEND // 128 // parts, (p + 1) * SEND // 128 // parts, narrow, 0)
        rows = pl.ds(p * SEND // parts, SEND // parts)
        store = pltpu.make_async_copy(o16.at[rows], out_hbm.at[rows], sem_out.at[p])
        store.start()
        stores.append(store)
    for store in stores:
        store.wait()


def pack(obs_values, obs_dest, obs_cell, obs_count):
    return pl.pallas_call(
        pack_kernel,
        out_shape=jax.ShapeDtypeStruct((SEND, CH), BF16),
        in_specs=[pl.BlockSpec(memory_space=pltpu.SMEM)] + [pl.BlockSpec(memory_space=pl.ANY)] * 3,
        out_specs=pl.BlockSpec(memory_space=pl.ANY),
        scratch_shapes=[
            pltpu.VMEM((32, 128), jnp.int32),
            pltpu.VMEM((32, 128), jnp.int32),
            pltpu.VMEM((ROWS, CH), BF16),
            pltpu.VMEM((SEND, CH), BF16),
            pltpu.VMEM((ROWS, CH), F32),
            pltpu.VMEM((SEND + 8, CH), F32),
            pltpu.VMEM((128, 128), jnp.int32),
            pltpu.SMEM((128, 128), jnp.int32),
            pltpu.SemaphoreType.DMA,
            pltpu.SemaphoreType.DMA((3,)),
            pltpu.SemaphoreType.DMA((3,)),
        ],
        compiler_params=pltpu.CompilerParams(vmem_limit_bytes=60 * 1024 * 1024),
        name="pack",
    )(obs_count, obs_dest.reshape(32, 128), obs_cell.reshape(32, 128), obs_values)


def grid_kernel(
    got_hbm, out_hbm, top_ref, bottom_ref, edge_ref,
    got_ref, out_ref, x32, acc, acc2, table_v, table_s, rowpair, colpair, edge32, sem, sem_in, sem_out,
):
    parts = 4
    fetches = []
    for p in range(parts):
        rows = pl.ds(p * SEND // parts, SEND // parts)
        fetch = pltpu.make_async_copy(got_hbm.at[rows], got_ref.at[rows], sem_in.at[p])
        fetch.start()
        fetches.append(fetch)

    def clear(i, c):
        acc[pl.ds(pl.multiple_of(i * 128, 128), 128), :] = jnp.zeros((128, CH), F32)
        acc2[pl.ds(pl.multiple_of(i * 128, 128), 128), :] = jnp.zeros((128, CH), F32)
        return c

    lax.fori_loop(0, (TRASH + TH * TW) // 128, clear, 0)

    def widen(i, c):
        rows = pl.ds(pl.multiple_of(i * 192, 192), 192)
        x32[rows, :] = got_ref[rows, :].astype(F32)
        return c

    for p in range(parts):
        fetches[p].wait()
        lax.fori_loop(p * SEND // 192 // parts, (p + 1) * SEND // 192 // parts, widen, 0)
    cells = jnp.concatenate([x32[s * BLK + CAP : s * BLK + CAP + 1, :] for s in range(DEV)], axis=0)
    swapped = pltpu.roll(cells, CAP, axis=1)
    lane = lax.broadcasted_iota(jnp.int32, (DEV, 128), 1)
    first = lane < CAP
    index = jnp.where(
        cells == 0.0, lane, cells.astype(jnp.int32) * TW + swapped.astype(jnp.int32)
    )
    index = jnp.where(first, index, -1)
    repeated = jnp.zeros((DEV, 128), jnp.bool_)
    for d in range(1, GROUP):
        same = (index == pltpu.roll(index, d, axis=1)) & (lane % GROUP >= d)
        repeated = repeated | same
    repeated = jnp.where(first & repeated, 1.0, 0.0).astype(BF16)
    groups = (
        lax.broadcasted_iota(jnp.int32, (128, 128), 0) // PART
        == (lax.broadcasted_iota(jnp.int32, (128, 128), 1) - CAP)
    ).astype(F32).astype(BF16)
    flags = jnp.dot(repeated, groups, preferred_element_type=F32)
    flags = (flags + pltpu.roll(flags, DEV // 2, axis=0)).astype(jnp.int32)
    table_v[...] = jnp.where(first, index, flags).T
    to_scalar = pltpu.make_async_copy(table_v, table_s, sem)
    to_scalar.start()

    half = DEV // 2
    firsth = lax.broadcasted_iota(jnp.int32, (half, 128), 1) < CAP
    rowpair[...] = jnp.where(firsth, cells[:half], swapped[half:])
    colpair[...] = jnp.where(firsth, swapped[:half], cells[half:])
    batch = 8
    col_ids = lax.broadcasted_iota(jnp.int32, (TW, 128), 0).astype(F32)
    row_ids = (lax.broadcasted_iota(jnp.int32, (128, 128), 0) + 1).astype(F32)

    def tally(i, total):
        at = [pl.ds(i * batch + k, 1) for k in range(batch)]
        col_hot = jnp.concatenate(
            [(col_ids == colpair[r, :]).astype(F32).astype(BF16) for r in at], axis=1
        )
        row_hot = jnp.concatenate(
            [(row_ids == rowpair[r, :]).astype(F32).astype(BF16) for r in at], axis=1
        )
        return total + lax.dot_general(
            col_hot, row_hot, (((1,), (1,)), ((), ())), preferred_element_type=F32
        )

    tallies = lax.fori_loop(0, half // batch, tally, jnp.zeros((TW, 128), F32))
    inverse = 1.0 / jnp.maximum(tallies, 1.0)

    to_scalar.wait()

    def source(s, c):
        pairs = ((acc, s), (acc2, s + half))
        for p in range(CAP // PART):
            clash = table_s.at[CAP + p][s]

            @pl.when(clash == 0)
            def _():
                for g in range(p * PART // GROUP, (p + 1) * PART // GROUP):
                    slots = range(g * GROUP, (g + 1) * GROUP)
                    index = [[pl.ds(table_s.at[k][t], 1) for k in slots] for _, t in pairs]
                    sums = [
                        [a[at, :] + x32[pl.ds(t * BLK + k, 1), :] for at, k in zip(ix, slots)]
                        for (a, t), ix in zip(pairs, index)
                    ]
                    for (a, _), ix, new in zip(pairs, index, sums):
                        for at, value in zip(ix, new):
                            a[at, :] = value

            @pl.when(clash != 0)
            def _():
                for k in range(p * PART, (p + 1) * PART):
                    for a, t in pairs:
                        at = pl.ds(table_s.at[k][t], 1)
                        a[at, :] = a[at, :] + x32[pl.ds(t * BLK + k, 1), :]

        return c

    lax.fori_loop(0, half, source, 0)
    stores = []
    for i in range(TH):
        scale = jnp.broadcast_to(inverse[:, i : i + 1], (TW, CH))
        rows = slice(TRASH + i * TW, TRASH + (i + 1) * TW)
        mean = (acc[rows, :] + acc2[rows, :]) * scale
        out_ref[i * TW : (i + 1) * TW, :] = mean.astype(BF16)
        if i == 0:
            top_ref[...] = mean.astype(BF16)
        if i >= TH - 2:
            bottom_ref[(i - TH + 2) * TW : (i - TH + 3) * TW, :] = mean.astype(BF16)
        edge32[0, i : i + 1, :] = mean[0:1]
        edge32[1, i : i + 1, :] = mean[239:240]
        edge32[2, i : i + 1, :] = mean[255:256]
        if (i + 1) % (TH // parts) == 0:
            p = i // (TH // parts)
            rows = pl.ds(p * (TH // parts) * TW, (TH // parts) * TW)
            store = pltpu.make_async_copy(out_ref.at[rows], out_hbm.at[rows], sem_out.at[p])
            store.start()
            stores.append(store)
    edge_ref[...] = edge32[...].astype(BF16)
    for store in stores:
        store.wait()


def to_grid(got):
    shapes = [(TH * TW, CH), (TW, CH), (2 * TW, CH), (3, TH, CH)]
    return pl.pallas_call(
        grid_kernel,
        out_shape=[jax.ShapeDtypeStruct(s, BF16) for s in shapes],
        in_specs=[pl.BlockSpec(memory_space=pl.ANY)],
        out_specs=[pl.BlockSpec(memory_space=pl.ANY)] + [pl.BlockSpec(memory_space=pltpu.VMEM)] * 3,
        scratch_shapes=[
            pltpu.VMEM((SEND, CH), BF16),
            pltpu.VMEM((TH * TW, CH), BF16),
            pltpu.VMEM((SEND, CH), F32),
            pltpu.VMEM((TRASH + TH * TW, CH), F32),
            pltpu.VMEM((TRASH + TH * TW, CH), F32),
            pltpu.VMEM((DEV, 128), jnp.int32),
            pltpu.SMEM((DEV, 128), jnp.int32),
            pltpu.VMEM((DEV // 2, 128), F32),
            pltpu.VMEM((DEV // 2, 128), F32),
            pltpu.VMEM((3, TH, CH), F32),
            pltpu.SemaphoreType.DMA,
            pltpu.SemaphoreType.DMA((4,)),
            pltpu.SemaphoreType.DMA((4,)),
        ],
        compiler_params=pltpu.CompilerParams(vmem_limit_bytes=52 * 1024 * 1024),
        name="to_grid",
    )(got)


def conv_kernel(
    band_ref, cell_hbm, north_hbm, south_hbm, own_hbm, west_hbm, east_hbm, w1_hbm, w2_hbm, out_ref,
    field, even, odd, own_ref, west_ref, east_ref, wcol, ecol, hcol, w1_ref, w2_ref, o32, sem,
):
    pairs = (
        (west_hbm, west_ref),
        (east_hbm, east_ref),
        (own_hbm, own_ref),
        (north_hbm, field.at[pl.ds(0, 2), pl.ds(1, 16)]),
        (south_hbm, field.at[2 + TH, pl.ds(1, 16)]),
        (cell_hbm, field.at[pl.ds(2, TH), pl.ds(1, 16)]),
        (w1_hbm, w1_ref),
        (w2_hbm, w2_ref),
    )
    fetches = [pltpu.make_async_copy(src, dst, sem.at[i]) for i, (src, dst) in enumerate(pairs)]
    for fetch in fetches:
        fetch.start()
    for fetch in fetches[:6]:
        fetch.wait()
    wcol[...] = west_ref[1].astype(F32)
    ecol[...] = east_ref[...].astype(F32)
    sub = lax.broadcasted_iota(jnp.int32, (16, CH), 0)

    def wrap(r, c):
        before = pltpu.roll(field[r, 16].astype(F32), 1, axis=0)
        field[r, 0] = jnp.where(sub == 0, wcol[pl.ds(r, 1), :], before).astype(BF16)
        after = pltpu.roll(field[r, 1].astype(F32), 15, axis=0)
        field[r, 17] = jnp.where(sub == 15, ecol[pl.ds(r, 1), :], after).astype(BF16)
        return c

    lax.fori_loop(0, TH + 3, wrap, 0, unroll=5)
    fetches[6].wait()

    taps = [west_ref[0].astype(F32), west_ref[1].astype(F32), own_ref[...].astype(F32)]
    lhs = jnp.concatenate([taps[b][a : a + 40] for a in range(3) for b in range(3)], axis=1)
    hcol[...] = gelu(jnp.dot(lhs.astype(BF16), w1_ref[...], preferred_element_type=F32))
    sub2 = lax.broadcasted_iota(jnp.int32, (16, HID), 0)

    def first(step, c):
        lhs = jnp.concatenate(
            [
                field[pl.ds(FIRST * step + a, FIRST), b : b + 16].reshape(FIRST * TW, CH)
                for a in range(3)
                for b in range(3)
            ],
            axis=1,
        )
        y = gelu(jnp.dot(lhs, w1_ref[...], preferred_element_type=F32))
        y16 = y.astype(BF16).reshape(FIRST, 8, 2, 16, HID)
        for r in range(FIRST):
            hr = FIRST * step + r
            odd[hr] = y16[r, :, 0]
            even[hr, 1:9] = y16[r, :, 1]
            before = pltpu.roll(y[r * TW + 240 : r * TW + 256], 1, axis=0)
            even[hr, 0] = jnp.where(sub2 == 0, hcol[pl.ds(hr, 1), :], before).astype(BF16)
        return c

    lax.fori_loop(0, (TH + 1) // FIRST, first, 0)

    @pl.when(band_ref[0] == 0)
    def _():
        even[0] = jnp.zeros((9, 16, HID), BF16)
        odd[0] = jnp.zeros((8, 16, HID), BF16)

    fetches[7].wait()

    def second(step, c):
        lhs = jnp.concatenate(
            [
                jnp.concatenate(
                    [
                        x.reshape(128, HID)
                        for a in range(3)
                        for x in (
                            even[2 * (SECOND * step + r) + a, 0:8],
                            odd[2 * (SECOND * step + r) + a],
                            even[2 * (SECOND * step + r) + a, 1:9],
                        )
                    ],
                    axis=1,
                )
                for r in range(SECOND)
            ],
            axis=0,
        )
        y = gelu(jnp.dot(lhs, w2_ref[...], preferred_element_type=F32))
        for r in range(SECOND):
            for h in range(2):
                for t in range(8):
                    o32[r, h, pl.ds(t, 16, stride=8), :] = y[
                        r * 128 + t * 16 : r * 128 + (t + 1) * 16, h * 128 : (h + 1) * 128
                    ]
            out_ref[SECOND * step + r] = jnp.concatenate([o32[r, 0], o32[r, 1]], axis=1).astype(BF16)
        return c

    lax.fori_loop(0, TH // 2 // SECOND, second, 0)


def convolve(band, cells, north, south, own, west, east, w1, w2):
    return pl.pallas_call(
        conv_kernel,
        out_shape=jax.ShapeDtypeStruct((TH // 2, TW // 2, HID), BF16),
        in_specs=[pl.BlockSpec(memory_space=pltpu.SMEM)] + [pl.BlockSpec(memory_space=pl.ANY)] * 8,
        out_specs=pl.BlockSpec(memory_space=pltpu.VMEM),
        scratch_shapes=[
            pltpu.VMEM((TH + 3, 18, 16, CH), BF16),
            pltpu.VMEM((TH + 1, 9, 16, HID), BF16),
            pltpu.VMEM((TH + 1, 8, 16, HID), BF16),
            pltpu.VMEM((COLS, CH), BF16),
            pltpu.VMEM((2, COLS, CH), BF16),
            pltpu.VMEM((COLS, CH), BF16),
            pltpu.VMEM((COLS, CH), F32),
            pltpu.VMEM((COLS, CH), F32),
            pltpu.VMEM((40, HID), F32),
            pltpu.VMEM((9 * CH, HID), BF16),
            pltpu.VMEM((9 * HID, HID), BF16),
            pltpu.VMEM((SECOND, 2, TW // 2, 128), F32),
            pltpu.SemaphoreType.DMA((8,)),
        ],
        compiler_params=pltpu.CompilerParams(vmem_limit_bytes=52 * 1024 * 1024),
        name="convolve",
    )(
        band, cells.reshape(TH, 16, 16, CH), north.reshape(2, 16, 16, CH), south.reshape(16, 16, CH),
        own, west, east, w1, w2,
    )


def body(obs_values, obs_dest, obs_cell, obs_count, conv_in, conv_down):
    lat = lax.axis_size("lat")
    lon = lax.axis_size("lon")
    send = pack(obs_values, obs_dest, obs_cell, obs_count)
    got = lax.all_to_all(
        send.reshape(DEV, BLK // 2, 2, CH), ("lat", "lon"), split_axis=0, concat_axis=0, tiled=True
    )
    cells, top, bottom, edge = to_grid(got.reshape(SEND, CH))
    north = lax.ppermute(bottom, "lat", [(i, i + 1) for i in range(lat - 1)])
    south = lax.ppermute(top, "lat", [(i + 1, i) for i in range(lat - 1)])
    north3 = north.reshape(2, TW, CH)
    full = jnp.stack(
        [
            jnp.concatenate(
                [north3[:, at], edge[e], south[at : at + 1], jnp.zeros((COLS - TH - 3, CH), BF16)]
            )
            for e, at in enumerate((0, 239, 255))
        ]
    )
    own = full[0]
    west = lax.ppermute(full[1:], "lon", [(i, (i + 1) % lon) for i in range(lon)])
    east = lax.ppermute(own, "lon", [((i + 1) % lon, i) for i in range(lon)])
    band = lax.axis_index("lat").astype(jnp.int32).reshape(1)
    return convolve(
        band, cells, north, south, own, west, east,
        conv_in.reshape(9 * CH, HID), conv_down.reshape(9 * HID, HID),
    )


def solution(mesh):
    placed = (
        P(("lat", "lon"), None),
        P(("lat", "lon"), None),
        P(("lat", "lon")),
        P(("lat", "lon")),
        P(),
        P(),
    )
    return jax.shard_map(
        body, mesh=mesh, in_specs=placed, out_specs=P("lat", "lon", None), check_vma=False
    )
```

```python
import functools

import jax
import jax.numpy as jnp
from jax import lax
from jax.experimental import pallas as pl
from jax.experimental.pallas import tpu as pltpu
from jax.sharding import PartitionSpec as P

TH = 32
TW = 256
CH = 128
HID = 256
DEV = 128
CAP = 64
ROWS = 4096
BLK = 66
SEND = DEV * BLK
TRASH = 256
GROUP = 8
PART = 64
FIRST = 11
SECOND = 8
COLS = 48
F32 = jnp.float32
BF16 = jnp.bfloat16


def gelu(x):
    inner = x * (0.7978845608028654 + 0.035677408136300125 * (x * x))
    return (0.5 * x) * (1.0 + jnp.tanh(inner))


def pack_kernel(
    count_ref, dest_hbm, cell_hbm, val_hbm, out_hbm,
    dest_ref, cell_ref, val_ref, o16, x32, o32, slot_v, slot_s, sem, sem_in, sem_out,
):
    fetches = [
        pltpu.make_async_copy(src, dst, sem_in.at[i])
        for i, (src, dst) in enumerate(((dest_hbm, dest_ref), (cell_hbm, cell_ref), (val_hbm, val_ref)))
    ]
    for fetch in fetches:
        fetch.start()
    count = count_ref[0]
    lane = lax.broadcasted_iota(jnp.int32, (1, 256), 1)
    dest_ids = lax.broadcasted_iota(jnp.int32, (DEV, 256), 0)
    pos_ids = lax.broadcasted_iota(jnp.int32, (CAP, 256), 0)
    upper = (
        lax.broadcasted_iota(jnp.int32, (256, 256), 0)
        < lax.broadcasted_iota(jnp.int32, (256, 256), 1)
    ).astype(F32).astype(BF16)
    fetches[0].wait()
    fetches[1].wait()
    carry = jnp.zeros((DEV, 1), F32)
    cells = jnp.zeros((DEV, 2 * CAP), F32)
    slots = []
    for a in range(ROWS // 256):
        dest = jnp.concatenate([dest_ref[2 * a : 2 * a + 1], dest_ref[2 * a + 1 : 2 * a + 2]], axis=1)
        cell = jnp.concatenate([cell_ref[2 * a : 2 * a + 1], cell_ref[2 * a + 1 : 2 * a + 2]], axis=1)
        live = (lane + 256 * a) < count
        dest_or = jnp.where(live, dest, DEV)
        hot = (dest_ids == dest_or).astype(F32)
        hot16 = hot.astype(BF16)
        before = jnp.dot(hot16, upper, preferred_element_type=F32) + carry
        carry = carry + jnp.sum(hot, axis=1, keepdims=True)
        pos = jnp.sum(hot * before, axis=0, keepdims=True).astype(jnp.int32)
        slot = jnp.where(live, dest * BLK + pos, SEND)
        slots += [slot[:, :128], slot[:, 128:]]
        high = (cell // TW + 1).astype(F32)
        low = ((cell % 16) * 16 + (cell % TW) // 16).astype(F32)
        pos_hot = pos_ids == pos
        coded = jnp.concatenate(
            [jnp.where(pos_hot, high, 0.0), jnp.where(pos_hot, low, 0.0)], axis=0
        ).astype(BF16)
        cells = cells + lax.dot_general(
            hot16, coded, (((1,), (1,)), ((), ())), preferred_element_type=F32
        )
    slot_v[...] = jnp.concatenate(slots, axis=0)
    to_scalar = pltpu.make_async_copy(slot_v, slot_s, sem)
    to_scalar.start()
    fetches[2].wait()

    def widen(i, c):
        rows = pl.ds(pl.multiple_of(i * 128, 128), 128)
        x32[rows, :] = val_ref[rows, :].astype(F32)
        return c

    lax.fori_loop(0, ROWS // 128, widen, 0)
    to_scalar.wait()

    def move(i, c):
        for k in range(ROWS // 128):
            o32[pl.ds(slot_s.at[k][i], 1), :] = x32[pl.ds(k * 128 + i, 1), :]
        return c

    lax.fori_loop(0, 128, move, 0)
    for d in range(DEV):
        o32[d * BLK + CAP : d * BLK + CAP + 1, :] = cells[d : d + 1, :]

    def narrow(i, c):
        rows = pl.ds(pl.multiple_of(i * 128, 128), 128)
        o16[rows, :] = o32[rows, :].astype(BF16)
        return c

    parts = 3
    stores = []
    for p in range(parts):
        lax.fori_loop(p * SEND // 128 // parts, (p + 1) * SEND // 128 // parts, narrow, 0)
        rows = pl.ds(p * SEND // parts, SEND // parts)
        store = pltpu.make_async_copy(o16.at[rows], out_hbm.at[rows], sem_out.at[p])
        store.start()
        stores.append(store)
    for store in stores:
        store.wait()


def pack(obs_values, obs_dest, obs_cell, obs_count):
    return pl.pallas_call(
        pack_kernel,
        out_shape=jax.ShapeDtypeStruct((SEND, CH), BF16),
        in_specs=[pl.BlockSpec(memory_space=pltpu.SMEM)] + [pl.BlockSpec(memory_space=pl.ANY)] * 3,
        out_specs=pl.BlockSpec(memory_space=pl.ANY),
        scratch_shapes=[
            pltpu.VMEM((32, 128), jnp.int32),
            pltpu.VMEM((32, 128), jnp.int32),
            pltpu.VMEM((ROWS, CH), BF16),
            pltpu.VMEM((SEND, CH), BF16),
            pltpu.VMEM((ROWS, CH), F32),
            pltpu.VMEM((SEND + 8, CH), F32),
            pltpu.VMEM((32, 128), jnp.int32),
            pltpu.SMEM((32, 128), jnp.int32),
            pltpu.SemaphoreType.DMA,
            pltpu.SemaphoreType.DMA((3,)),
            pltpu.SemaphoreType.DMA((3,)),
        ],
        compiler_params=pltpu.CompilerParams(vmem_limit_bytes=60 * 1024 * 1024),
        name="pack",
    )(obs_count, obs_dest.reshape(32, 128), obs_cell.reshape(32, 128), obs_values)


def grid_kernel(
    got_hbm, out_hbm, top_ref, bottom_ref, edge_ref,
    got_ref, out_ref, x32, acc, acc2, table_v, table_s, rowpair, colpair, inverse, edge32, sem, sem_in, sem_out,
):
    parts = 4
    fetches = []
    for p in range(parts):
        rows = pl.ds(p * SEND // parts, SEND // parts)
        fetch = pltpu.make_async_copy(got_hbm.at[rows], got_ref.at[rows], sem_in.at[p])
        fetch.start()
        fetches.append(fetch)

    def clear(i, c):
        acc[pl.ds(pl.multiple_of(i * 128, 128), 128), :] = jnp.zeros((128, CH), F32)
        acc2[pl.ds(pl.multiple_of(i * 128, 128), 128), :] = jnp.zeros((128, CH), F32)
        return c

    lax.fori_loop(0, (TRASH + TH * TW) // 128, clear, 0)

    def widen(i, c):
        rows = pl.ds(pl.multiple_of(i * 192, 192), 192)
        x32[rows, :] = got_ref[rows, :].astype(F32)
        return c

    for p in range(parts):
        fetches[p].wait()
        lax.fori_loop(p * SEND // 192 // parts, (p + 1) * SEND // 192 // parts, widen, 0)
    cells = x32[pl.ds(CAP, DEV, stride=BLK), :]
    swapped = pltpu.roll(cells, CAP, axis=1)
    lane = lax.broadcasted_iota(jnp.int32, (DEV, 128), 1)
    first = lane < CAP
    index = jnp.where(
        cells == 0.0, lane, cells.astype(jnp.int32) * TW + swapped.astype(jnp.int32)
    )
    index = jnp.where(first, index, -1)
    repeated = jnp.zeros((DEV, 128), jnp.bool_)
    for d in range(1, GROUP):
        same = (index == pltpu.roll(index, d, axis=1)) & (lane % GROUP >= d)
        repeated = repeated | same
    repeated = jnp.where(first & repeated, 1.0, 0.0).astype(BF16)
    groups = (
        lax.broadcasted_iota(jnp.int32, (128, 128), 0) // PART
        == (lax.broadcasted_iota(jnp.int32, (128, 128), 1) - CAP)
    ).astype(F32).astype(BF16)
    flags = jnp.dot(repeated, groups, preferred_element_type=F32)
    flags = (flags + pltpu.roll(flags, DEV // 2, axis=0)).astype(jnp.int32)
    table_v[...] = jnp.where(first, index, flags).T
    to_scalar = []
    for n, rows in enumerate((pl.ds(CAP, 8), pl.ds(0, CAP))):
        to_scalar.append(pltpu.make_async_copy(table_v.at[rows], table_s.at[rows], sem.at[n]))
        to_scalar[n].start()

    half = DEV // 2
    firsth = lax.broadcasted_iota(jnp.int32, (half, 128), 1) < CAP
    rowpair[...] = jnp.where(firsth, cells[:half], swapped[half:])
    colpair[...] = jnp.where(firsth, swapped[:half], cells[half:])
    batch = 8
    col_ids = lax.broadcasted_iota(jnp.int32, (TW, 128), 0).astype(F32)
    row_ids = (lax.broadcasted_iota(jnp.int32, (128, 128), 0) + 1).astype(F32)

    def tally(i, total):
        at = [pl.ds(i * batch + k, 1) for k in range(batch)]
        col_hot = jnp.concatenate(
            [(col_ids == colpair[r, :]).astype(F32).astype(BF16) for r in at], axis=1
        )
        row_hot = jnp.concatenate(
            [(row_ids == rowpair[r, :]).astype(F32).astype(BF16) for r in at], axis=1
        )
        return total + lax.dot_general(
            col_hot, row_hot, (((1,), (1,)), ((), ())), preferred_element_type=F32
        )

    tallies = lax.fori_loop(0, half // batch, tally, jnp.zeros((TW, 128), F32))
    inverse[...] = 1.0 / jnp.maximum(tallies, 1.0)

    to_scalar[0].wait()
    for p in range(CAP // PART):
        to_scalar[1 + p].wait()

        def source(s, c):
            pairs = ((acc, s), (acc2, s + half))
            clash = table_s.at[CAP + p][s]

            @pl.when(clash == 0)
            def _():
                for g in range(p * PART // GROUP, (p + 1) * PART // GROUP):
                    slots = range(g * GROUP, (g + 1) * GROUP)
                    index = [[pl.ds(table_s.at[k][t], 1) for k in slots] for _, t in pairs]
                    sums = [
                        [a[at, :] + x32[pl.ds(t * BLK + k, 1), :] for at, k in zip(ix, slots)]
                        for (a, t), ix in zip(pairs, index)
                    ]
                    for (a, _), ix, new in zip(pairs, index, sums):
                        for at, value in zip(ix, new):
                            a[at, :] = value

            @pl.when(clash != 0)
            def _():
                for k in range(p * PART, (p + 1) * PART):
                    for a, t in pairs:
                        at = pl.ds(table_s.at[k][t], 1)
                        a[at, :] = a[at, :] + x32[pl.ds(t * BLK + k, 1), :]

            return c

        lax.fori_loop(0, half, source, 0)

    span = TH // parts

    def normalise(p, c):
        scales = inverse[...]
        for k in range(span):
            i = p * span + k
            rows = pl.ds(pl.multiple_of(TRASH + i * TW, TW), TW)
            mean = (acc[rows, :] + acc2[rows, :]) * jnp.broadcast_to(scales[:, k : k + 1], (TW, CH))
            out_ref[pl.ds(pl.multiple_of(i * TW, TW), TW), :] = mean.astype(BF16)
            for e, at in enumerate((0, 239, 255)):
                edge32[e, pl.ds(i, 1), :] = mean[at : at + 1]
        inverse[...] = pltpu.roll(scales, 128 - span, axis=1)
        rows = pl.ds(pl.multiple_of(p * span * TW, TW), span * TW)
        pltpu.make_async_copy(out_ref.at[rows], out_hbm.at[rows], sem_out.at[p]).start()
        return c

    lax.fori_loop(0, parts, normalise, 0)
    top_ref[...] = out_ref[:TW, :]
    bottom_ref[...] = out_ref[(TH - 2) * TW :, :]
    edge_ref[...] = edge32[...].astype(BF16)
    for p in range(parts):
        rows = pl.ds(p * span * TW, span * TW)
        pltpu.make_async_copy(out_ref.at[rows], out_hbm.at[rows], sem_out.at[p]).wait()


def to_grid(got):
    shapes = [(TH * TW, CH), (TW, CH), (2 * TW, CH), (3, TH, CH)]
    return pl.pallas_call(
        grid_kernel,
        out_shape=[jax.ShapeDtypeStruct(s, BF16) for s in shapes],
        in_specs=[pl.BlockSpec(memory_space=pl.ANY)],
        out_specs=[pl.BlockSpec(memory_space=pl.ANY)] + [pl.BlockSpec(memory_space=pltpu.VMEM)] * 3,
        scratch_shapes=[
            pltpu.VMEM((SEND, CH), BF16),
            pltpu.VMEM((TH * TW, CH), BF16),
            pltpu.VMEM((SEND, CH), F32),
            pltpu.VMEM((TRASH + TH * TW, CH), F32),
            pltpu.VMEM((TRASH + TH * TW, CH), F32),
            pltpu.VMEM((DEV, 128), jnp.int32),
            pltpu.SMEM((CAP + 8, 128), jnp.int32),
            pltpu.VMEM((DEV // 2, 128), F32),
            pltpu.VMEM((DEV // 2, 128), F32),
            pltpu.VMEM((TW, 128), F32),
            pltpu.VMEM((3, TH, CH), F32),
            pltpu.SemaphoreType.DMA((2,)),
            pltpu.SemaphoreType.DMA((4,)),
            pltpu.SemaphoreType.DMA((4,)),
        ],
        compiler_params=pltpu.CompilerParams(vmem_limit_bytes=52 * 1024 * 1024),
        name="to_grid",
    )(got)


def conv_kernel(
    band_ref, cell_hbm, north_hbm, south_hbm, own_hbm, west_hbm, east_hbm, w1_hbm, w2_hbm, out_hbm,
    field, even, odd, own_ref, west_ref, east_ref, wcol, ecol, hcol, w1_ref, w2_ref, o32, out_ref, sem, sem_out,
):
    steps = (TH + 1) // FIRST
    pairs = [
        (west_hbm, west_ref),
        (east_hbm, east_ref),
        (own_hbm, own_ref),
        (w1_hbm, w1_ref),
        (north_hbm, field.at[pl.ds(0, 2), pl.ds(1, 16)]),
        (south_hbm, field.at[2 + TH, pl.ds(1, 16)]),
        (w2_hbm, w2_ref),
    ]
    for i in range(steps):
        size = min(TH, (i + 1) * FIRST) - i * FIRST
        pairs.append(
            (cell_hbm.at[pl.ds(i * FIRST, size)], field.at[pl.ds(2 + i * FIRST, size), pl.ds(1, 16)])
        )
    fetches = [pltpu.make_async_copy(src, dst, sem.at[i]) for i, (src, dst) in enumerate(pairs)]
    for fetch in fetches:
        fetch.start()
    for fetch in fetches[:6]:
        fetch.wait()
    wcol[...] = west_ref[1].astype(F32)
    ecol[...] = east_ref[...].astype(F32)
    sub = lax.broadcasted_iota(jnp.int32, (16, CH), 0)

    def wrap(r, c):
        before = pltpu.roll(field[r, 16].astype(F32), 1, axis=0)
        field[r, 0] = jnp.where(sub == 0, wcol[pl.ds(r, 1), :], before).astype(BF16)
        after = pltpu.roll(field[r, 1].astype(F32), 15, axis=0)
        field[r, 17] = jnp.where(sub == 15, ecol[pl.ds(r, 1), :], after).astype(BF16)
        return c

    taps = [west_ref[0].astype(F32), west_ref[1].astype(F32), own_ref[...].astype(F32)]
    lhs = jnp.concatenate([taps[b][a : a + 40] for a in range(3) for b in range(3)], axis=1)
    hcol[...] = gelu(jnp.dot(lhs.astype(BF16), w1_ref[...], preferred_element_type=F32))
    lax.fori_loop(0, 2, wrap, 0)
    sub2 = lax.broadcasted_iota(jnp.int32, (16, HID), 0)

    def first(step, c):
        for i in range(steps):
            pl.when(step == i)(fetches[7 + i].wait)
        lax.fori_loop(2 + FIRST * step, 2 + FIRST * (step + 1), wrap, 0)
        lhs = jnp.concatenate(
            [
                field[pl.ds(FIRST * step + a, FIRST), b : b + 16].reshape(FIRST * TW, CH)
                for a in range(3)
                for b in range(3)
            ],
            axis=1,
        )
        y = gelu(jnp.dot(lhs, w1_ref[...], preferred_element_type=F32))
        y16 = y.astype(BF16).reshape(FIRST, 8, 2, 16, HID)
        for r in range(FIRST):
            hr = FIRST * step + r
            odd[hr] = y16[r, :, 0]
            even[hr, 1:9] = y16[r, :, 1]
            before = pltpu.roll(y[r * TW + 240 : r * TW + 256], 1, axis=0)
            even[hr, 0] = jnp.where(sub2 == 0, hcol[pl.ds(hr, 1), :], before).astype(BF16)
        return c

    lax.fori_loop(0, (TH + 1) // FIRST, first, 0)

    @pl.when(band_ref[0] == 0)
    def _():
        even[0] = jnp.zeros((9, 16, HID), BF16)
        odd[0] = jnp.zeros((8, 16, HID), BF16)

    fetches[6].wait()

    def second(step, c):
        lhs = jnp.concatenate(
            [
                jnp.concatenate(
                    [
                        x.reshape(128, HID)
                        for a in range(3)
                        for x in (
                            even[2 * (SECOND * step + r) + a, 0:8],
                            odd[2 * (SECOND * step + r) + a],
                            even[2 * (SECOND * step + r) + a, 1:9],
                        )
                    ],
                    axis=1,
                )
                for r in range(SECOND)
            ],
            axis=0,
        )
        y = gelu(jnp.dot(lhs, w2_ref[...], preferred_element_type=F32))
        for r in range(SECOND):
            for h in range(2):
                for t in range(8):
                    o32[r, h, pl.ds(t, 16, stride=8), :] = y[
                        r * 128 + t * 16 : r * 128 + (t + 1) * 16, h * 128 : (h + 1) * 128
                    ]
            out_ref[SECOND * step + r] = jnp.concatenate([o32[r, 0], o32[r, 1]], axis=1).astype(BF16)
        rows = pl.ds(SECOND * step, SECOND)
        pltpu.make_async_copy(out_ref.at[rows], out_hbm.at[rows], sem_out.at[step]).start()
        return c

    lax.fori_loop(0, TH // 2 // SECOND, second, 0)
    for i in range(TH // 2 // SECOND):
        rows = pl.ds(SECOND * i, SECOND)
        pltpu.make_async_copy(out_ref.at[rows], out_hbm.at[rows], sem_out.at[i]).wait()


def convolve(band, cells, north, south, own, west, east, w1, w2):
    return pl.pallas_call(
        conv_kernel,
        out_shape=jax.ShapeDtypeStruct((TH // 2, TW // 2, HID), BF16),
        in_specs=[pl.BlockSpec(memory_space=pltpu.SMEM)] + [pl.BlockSpec(memory_space=pl.ANY)] * 8,
        out_specs=pl.BlockSpec(memory_space=pl.ANY),
        scratch_shapes=[
            pltpu.VMEM((TH + 3, 18, 16, CH), BF16),
            pltpu.VMEM((TH + 1, 9, 16, HID), BF16),
            pltpu.VMEM((TH + 1, 8, 16, HID), BF16),
            pltpu.VMEM((COLS, CH), BF16),
            pltpu.VMEM((2, COLS, CH), BF16),
            pltpu.VMEM((COLS, CH), BF16),
            pltpu.VMEM((COLS, CH), F32),
            pltpu.VMEM((COLS, CH), F32),
            pltpu.VMEM((40, HID), F32),
            pltpu.VMEM((9 * CH, HID), BF16),
            pltpu.VMEM((9 * HID, HID), BF16),
            pltpu.VMEM((SECOND, 2, TW // 2, 128), F32),
            pltpu.VMEM((TH // 2, TW // 2, HID), BF16),
            pltpu.SemaphoreType.DMA((7 + (TH + 1) // FIRST,)),
            pltpu.SemaphoreType.DMA((TH // 2 // SECOND,)),
        ],
        compiler_params=pltpu.CompilerParams(vmem_limit_bytes=52 * 1024 * 1024),
        name="convolve",
    )(
        band, cells.reshape(TH, 16, 16, CH), north.reshape(2, 16, 16, CH), south.reshape(16, 16, CH),
        own, west, east, w1, w2,
    )


def body(obs_values, obs_dest, obs_cell, obs_count, conv_in, conv_down):
    lat = lax.axis_size("lat")
    lon = lax.axis_size("lon")
    send = pack(obs_values, obs_dest, obs_cell, obs_count)
    got = lax.all_to_all(
        send.reshape(DEV, BLK // 2, 2, CH), ("lat", "lon"), split_axis=0, concat_axis=0, tiled=True
    )
    cells, top, bottom, edge = to_grid(got.reshape(SEND, CH))
    north = lax.ppermute(bottom, "lat", [(i, i + 1) for i in range(lat - 1)])
    south = lax.ppermute(top, "lat", [(i + 1, i) for i in range(lat - 1)])
    north3 = north.reshape(2, TW, CH)
    full = jnp.stack(
        [
            jnp.concatenate(
                [north3[:, at], edge[e], south[at : at + 1], jnp.zeros((COLS - TH - 3, CH), BF16)]
            )
            for e, at in enumerate((0, 239, 255))
        ]
    )
    own = full[0]
    west = lax.ppermute(full[1:], "lon", [(i, (i + 1) % lon) for i in range(lon)])
    east = lax.ppermute(own, "lon", [((i + 1) % lon, i) for i in range(lon)])
    band = lax.axis_index("lat").astype(jnp.int32).reshape(1)
    return convolve(
        band, cells, north, south, own, west, east,
        conv_in.reshape(9 * CH, HID), conv_down.reshape(9 * HID, HID),
    )


def solution(mesh):
    placed = (
        P(("lat", "lon"), None),
        P(("lat", "lon"), None),
        P(("lat", "lon")),
        P(("lat", "lon")),
        P(),
        P(),
    )
    return jax.shard_map(
        body, mesh=mesh, in_specs=placed, out_specs=P("lat", "lon", None), check_vma=False
    )
```

```python
import functools

import jax
import jax.numpy as jnp
from jax import lax
from jax.experimental import pallas as pl
from jax.experimental.pallas import tpu as pltpu
from jax.sharding import PartitionSpec as P

TH = 32
TW = 256
CH = 128
HID = 256
DEV = 128
CAP = 64
ROWS = 4096
BLK = 66
SEND = DEV * BLK
TRASH = 256
GROUP = 8
FIRST = 11
SECOND = 8
COLS = 48
F32 = jnp.float32
BF16 = jnp.bfloat16


def gelu(x):
    inner = x * (0.7978845608028654 + 0.035677408136300125 * (x * x))
    return (0.5 * x) * (1.0 + jnp.tanh(inner))


def pack_kernel(
    count_ref, dest_hbm, cell_hbm, val_hbm, out_hbm,
    dest_ref, cell_ref, val_ref, o16, x32, o32, slot_v, slot_s, sem, sem_in, sem_out,
):
    fetches = [
        pltpu.make_async_copy(src, dst, sem_in.at[i])
        for i, (src, dst) in enumerate(((dest_hbm, dest_ref), (cell_hbm, cell_ref), (val_hbm, val_ref)))
    ]
    for fetch in fetches:
        fetch.start()
    count = count_ref[0]
    lane = lax.broadcasted_iota(jnp.int32, (1, 256), 1)
    dest_ids = lax.broadcasted_iota(jnp.int32, (DEV, 256), 0)
    pos_ids = lax.broadcasted_iota(jnp.int32, (CAP, 256), 0)
    upper = (
        lax.broadcasted_iota(jnp.int32, (256, 256), 0)
        < lax.broadcasted_iota(jnp.int32, (256, 256), 1)
    ).astype(F32).astype(BF16)
    fetches[0].wait()
    fetches[1].wait()
    carry = jnp.zeros((DEV, 1), F32)
    cells = jnp.zeros((DEV, 2 * CAP), F32)
    slots = []
    for a in range(ROWS // 256):
        dest = jnp.concatenate([dest_ref[2 * a : 2 * a + 1], dest_ref[2 * a + 1 : 2 * a + 2]], axis=1)
        cell = jnp.concatenate([cell_ref[2 * a : 2 * a + 1], cell_ref[2 * a + 1 : 2 * a + 2]], axis=1)
        live = (lane + 256 * a) < count
        dest_or = jnp.where(live, dest, DEV)
        hot = (dest_ids == dest_or).astype(F32)
        hot16 = hot.astype(BF16)
        before = jnp.dot(hot16, upper, preferred_element_type=F32) + carry
        carry = carry + jnp.sum(hot, axis=1, keepdims=True)
        pos = jnp.sum(hot * before, axis=0, keepdims=True).astype(jnp.int32)
        slot = jnp.where(live, dest * BLK + pos, SEND)
        slots += [slot[:, :128], slot[:, 128:]]
        high = (cell // TW + 1).astype(F32)
        low = ((cell % 16) * 16 + (cell % TW) // 16).astype(F32)
        pos_hot = pos_ids == pos
        coded = jnp.concatenate(
            [jnp.where(pos_hot, high, 0.0), jnp.where(pos_hot, low, 0.0)], axis=0
        ).astype(BF16)
        cells = cells + lax.dot_general(
            hot16, coded, (((1,), (1,)), ((), ())), preferred_element_type=F32
        )
    slot_v[...] = jnp.concatenate(slots, axis=0)
    to_scalar = pltpu.make_async_copy(slot_v, slot_s, sem)
    to_scalar.start()
    fetches[2].wait()

    def widen(i, c):
        rows = pl.ds(pl.multiple_of(i * 128, 128), 128)
        x32[rows, :] = val_ref[rows, :].astype(F32)
        return c

    lax.fori_loop(0, ROWS // 128, widen, 0)
    to_scalar.wait()

    def move(i, c):
        for k in range(ROWS // 128):
            o32[pl.ds(slot_s.at[k][i], 1), :] = x32[pl.ds(k * 128 + i, 1), :]
        return c

    lax.fori_loop(0, 128, move, 0)
    for d in range(DEV):
        o32[d * BLK + CAP : d * BLK + CAP + 1, :] = cells[d : d + 1, :]

    def narrow(i, c):
        rows = pl.ds(pl.multiple_of(i * 128, 128), 128)
        o16[rows, :] = o32[rows, :].astype(BF16)
        return c

    parts = 3
    stores = []
    for p in range(parts):
        lax.fori_loop(p * SEND // 128 // parts, (p + 1) * SEND // 128 // parts, narrow, 0)
        rows = pl.ds(p * SEND // parts, SEND // parts)
        store = pltpu.make_async_copy(o16.at[rows], out_hbm.at[rows], sem_out.at[p])
        store.start()
        stores.append(store)
    for store in stores:
        store.wait()


def pack(obs_values, obs_dest, obs_cell, obs_count):
    return pl.pallas_call(
        pack_kernel,
        out_shape=jax.ShapeDtypeStruct((SEND, CH), BF16),
        in_specs=[pl.BlockSpec(memory_space=pltpu.SMEM)] + [pl.BlockSpec(memory_space=pl.ANY)] * 3,
        out_specs=pl.BlockSpec(memory_space=pl.ANY),
        scratch_shapes=[
            pltpu.VMEM((32, 128), jnp.int32),
            pltpu.VMEM((32, 128), jnp.int32),
            pltpu.VMEM((ROWS, CH), BF16),
            pltpu.VMEM((SEND, CH), BF16),
            pltpu.VMEM((ROWS, CH), F32),
            pltpu.VMEM((SEND + 8, CH), F32),
            pltpu.VMEM((32, 128), jnp.int32),
            pltpu.SMEM((32, 128), jnp.int32),
            pltpu.SemaphoreType.DMA,
            pltpu.SemaphoreType.DMA((3,)),
            pltpu.SemaphoreType.DMA((3,)),
        ],
        compiler_params=pltpu.CompilerParams(vmem_limit_bytes=60 * 1024 * 1024),
        name="pack",
    )(obs_count, obs_dest.reshape(32, 128), obs_cell.reshape(32, 128), obs_values)


def grid_kernel(
    got_hbm, out_hbm, top_ref, bottom_ref, edge_ref,
    got_ref, out_ref, x32, acc, acc2, table_v, table_s, rowpair, colpair, inverse, edge32, sem, sem_in, sem_out,
):
    parts = 4
    fetches = []
    for p in range(parts):
        rows = pl.ds(p * SEND // parts, SEND // parts)
        fetch = pltpu.make_async_copy(got_hbm.at[rows], got_ref.at[rows], sem_in.at[p])
        fetch.start()
        fetches.append(fetch)

    def clear(i, c):
        acc[pl.ds(pl.multiple_of(i * 128, 128), 128), :] = jnp.zeros((128, CH), F32)
        acc2[pl.ds(pl.multiple_of(i * 128, 128), 128), :] = jnp.zeros((128, CH), F32)
        return c

    lax.fori_loop(0, (TRASH + TH * TW) // 128, clear, 0)

    def widen(i, c):
        rows = pl.ds(pl.multiple_of(i * 192, 192), 192)
        x32[rows, :] = got_ref[rows, :].astype(F32)
        return c

    for p in range(parts):
        fetches[p].wait()
        lax.fori_loop(p * SEND // 192 // parts, (p + 1) * SEND // 192 // parts, widen, 0)
    cells = x32[pl.ds(CAP, DEV, stride=BLK), :]
    swapped = pltpu.roll(cells, CAP, axis=1)
    lane = lax.broadcasted_iota(jnp.int32, (DEV, 128), 1)
    first = lane < CAP
    index = jnp.where(
        cells == 0.0, lane, cells.astype(jnp.int32) * TW + swapped.astype(jnp.int32)
    )
    index = jnp.where(first, index, -1)
    repeated = jnp.zeros((DEV, 128), jnp.bool_)
    for d in range(1, GROUP):
        same = (index == pltpu.roll(index, d, axis=1)) & (lane % GROUP >= d)
        repeated = repeated | same
    repeated = jnp.where(first & repeated, 1.0, 0.0).astype(BF16)
    slot = lax.broadcasted_iota(jnp.int32, (128, 128), 0)
    kind = lax.broadcasted_iota(jnp.int32, (128, 128), 1) - CAP
    groups = ((kind == 0) | (slot // GROUP == kind - 8)).astype(F32).astype(BF16)
    flags = jnp.dot(repeated, groups, preferred_element_type=F32)
    flags = (flags + pltpu.roll(flags, DEV // 2, axis=0)).astype(jnp.int32)
    table_v[...] = jnp.where(first, index, flags).T
    to_scalar = []
    for n, rows in enumerate((pl.ds(CAP, 16), pl.ds(0, CAP))):
        to_scalar.append(pltpu.make_async_copy(table_v.at[rows], table_s.at[rows], sem.at[n]))
        to_scalar[n].start()

    half = DEV // 2
    firsth = lax.broadcasted_iota(jnp.int32, (half, 128), 1) < CAP
    rowpair[...] = jnp.where(firsth, cells[:half], swapped[half:])
    colpair[...] = jnp.where(firsth, swapped[:half], cells[half:])
    batch = 8
    col_ids = lax.broadcasted_iota(jnp.int32, (TW, 128), 0).astype(F32)
    row_ids = (lax.broadcasted_iota(jnp.int32, (128, 128), 0) + 1).astype(F32)

    def tally(i, total):
        at = [pl.ds(i * batch + k, 1) for k in range(batch)]
        col_hot = jnp.concatenate(
            [(col_ids == colpair[r, :]).astype(F32).astype(BF16) for r in at], axis=1
        )
        row_hot = jnp.concatenate(
            [(row_ids == rowpair[r, :]).astype(F32).astype(BF16) for r in at], axis=1
        )
        return total + lax.dot_general(
            col_hot, row_hot, (((1,), (1,)), ((), ())), preferred_element_type=F32
        )

    tallies = lax.fori_loop(0, half // batch, tally, jnp.zeros((TW, 128), F32))
    inverse[...] = 1.0 / jnp.maximum(tallies, 1.0)

    to_scalar[0].wait()
    to_scalar[1].wait()

    def source(s, c):
        pairs = ((acc, s), (acc2, s + half))

        def add_group(g):
            slots = range(g * GROUP, (g + 1) * GROUP)
            index = [[pl.ds(table_s.at[k][t], 1) for k in slots] for _, t in pairs]
            sums = [
                [a[at, :] + x32[pl.ds(t * BLK + k, 1), :] for at, k in zip(ix, slots)]
                for (a, t), ix in zip(pairs, index)
            ]
            for (a, _), ix, new in zip(pairs, index, sums):
                for at, value in zip(ix, new):
                    a[at, :] = value

        def add_singly(g):
            for k in range(g * GROUP, (g + 1) * GROUP):
                for a, t in pairs:
                    at = pl.ds(table_s.at[k][t], 1)
                    a[at, :] = a[at, :] + x32[pl.ds(t * BLK + k, 1), :]

        clash = table_s.at[CAP][s]

        @pl.when(clash == 0)
        def _():
            for g in range(CAP // GROUP):
                add_group(g)

        @pl.when(clash != 0)
        def _():
            for g in range(CAP // GROUP):
                here = table_s.at[CAP + 8 + g][s]
                pl.when(here == 0)(lambda: add_group(g))
                pl.when(here != 0)(lambda: add_singly(g))

        return c

    lax.fori_loop(0, half, source, 0)

    span = TH // parts

    def normalise(p, c):
        scales = inverse[...]
        for k in range(span):
            i = p * span + k
            rows = pl.ds(pl.multiple_of(TRASH + i * TW, TW), TW)
            mean = (acc[rows, :] + acc2[rows, :]) * jnp.broadcast_to(scales[:, k : k + 1], (TW, CH))
            out_ref[pl.ds(pl.multiple_of(i * TW, TW), TW), :] = mean.astype(BF16)
            for e, at in enumerate((0, 239, 255)):
                edge32[e, pl.ds(i, 1), :] = mean[at : at + 1]
        inverse[...] = pltpu.roll(scales, 128 - span, axis=1)
        rows = pl.ds(pl.multiple_of(p * span * TW, TW), span * TW)
        pltpu.make_async_copy(out_ref.at[rows], out_hbm.at[rows], sem_out.at[p]).start()
        return c

    lax.fori_loop(0, parts, normalise, 0)
    top_ref[...] = out_ref[:TW, :]
    bottom_ref[...] = out_ref[(TH - 2) * TW :, :]
    edge_ref[...] = edge32[...].astype(BF16)
    for p in range(parts):
        rows = pl.ds(p * span * TW, span * TW)
        pltpu.make_async_copy(out_ref.at[rows], out_hbm.at[rows], sem_out.at[p]).wait()


def to_grid(got):
    shapes = [(TH * TW, CH), (TW, CH), (2 * TW, CH), (3, TH, CH)]
    return pl.pallas_call(
        grid_kernel,
        out_shape=[jax.ShapeDtypeStruct(s, BF16) for s in shapes],
        in_specs=[pl.BlockSpec(memory_space=pl.ANY)],
        out_specs=[pl.BlockSpec(memory_space=pl.ANY)] + [pl.BlockSpec(memory_space=pltpu.VMEM)] * 3,
        scratch_shapes=[
            pltpu.VMEM((SEND, CH), BF16),
            pltpu.VMEM((TH * TW, CH), BF16),
            pltpu.VMEM((SEND, CH), F32),
            pltpu.VMEM((TRASH + TH * TW, CH), F32),
            pltpu.VMEM((TRASH + TH * TW, CH), F32),
            pltpu.VMEM((DEV, 128), jnp.int32),
            pltpu.SMEM((CAP + 16, 128), jnp.int32),
            pltpu.VMEM((DEV // 2, 128), F32),
            pltpu.VMEM((DEV // 2, 128), F32),
            pltpu.VMEM((TW, 128), F32),
            pltpu.VMEM((3, TH, CH), F32),
            pltpu.SemaphoreType.DMA((2,)),
            pltpu.SemaphoreType.DMA((4,)),
            pltpu.SemaphoreType.DMA((4,)),
        ],
        compiler_params=pltpu.CompilerParams(vmem_limit_bytes=52 * 1024 * 1024),
        name="to_grid",
    )(got)


def conv_kernel(
    band_ref, cell_hbm, north_hbm, south_hbm, own_hbm, west_hbm, east_hbm, w1_hbm, w2_hbm, out_hbm,
    field, even, odd, own_ref, west_ref, east_ref, wcol, ecol, hcol, w1_ref, w2_ref, o32, out_ref, sem, sem_out,
):
    steps = (TH + 1) // FIRST
    pairs = [
        (west_hbm, west_ref),
        (east_hbm, east_ref),
        (own_hbm, own_ref),
        (w1_hbm, w1_ref),
        (north_hbm, field.at[pl.ds(0, 2), pl.ds(1, 16)]),
        (south_hbm, field.at[2 + TH, pl.ds(1, 16)]),
        (w2_hbm, w2_ref),
    ]
    for i in range(steps):
        size = min(TH, (i + 1) * FIRST) - i * FIRST
        pairs.append(
            (cell_hbm.at[pl.ds(i * FIRST, size)], field.at[pl.ds(2 + i * FIRST, size), pl.ds(1, 16)])
        )
    fetches = [pltpu.make_async_copy(src, dst, sem.at[i]) for i, (src, dst) in enumerate(pairs)]
    for fetch in fetches:
        fetch.start()
    for fetch in fetches[:6]:
        fetch.wait()
    wcol[...] = west_ref[1].astype(F32)
    ecol[...] = east_ref[...].astype(F32)
    sub = lax.broadcasted_iota(jnp.int32, (16, CH), 0)

    def wrap(r, c):
        before = pltpu.roll(field[r, 16].astype(F32), 1, axis=0)
        field[r, 0] = jnp.where(sub == 0, wcol[pl.ds(r, 1), :], before).astype(BF16)
        after = pltpu.roll(field[r, 1].astype(F32), 15, axis=0)
        field[r, 17] = jnp.where(sub == 15, ecol[pl.ds(r, 1), :], after).astype(BF16)
        return c

    taps = [west_ref[0].astype(F32), west_ref[1].astype(F32), own_ref[...].astype(F32)]
    lhs = jnp.concatenate([taps[b][a : a + 40] for a in range(3) for b in range(3)], axis=1)
    hcol[...] = gelu(jnp.dot(lhs.astype(BF16), w1_ref[...], preferred_element_type=F32))
    lax.fori_loop(0, 2, wrap, 0)
    sub2 = lax.broadcasted_iota(jnp.int32, (16, HID), 0)

    def first(step, c):
        for i in range(steps):
            pl.when(step == i)(fetches[7 + i].wait)
        lax.fori_loop(2 + FIRST * step, 2 + FIRST * (step + 1), wrap, 0)
        lhs = jnp.concatenate(
            [
                field[pl.ds(FIRST * step + a, FIRST), b : b + 16].reshape(FIRST * TW, CH)
                for a in range(3)
                for b in range(3)
            ],
            axis=1,
        )
        y = gelu(jnp.dot(lhs, w1_ref[...], preferred_element_type=F32))
        y16 = y.astype(BF16).reshape(FIRST, 8, 2, 16, HID)
        for r in range(FIRST):
            hr = FIRST * step + r
            odd[hr] = y16[r, :, 0]
            even[hr, 1:9] = y16[r, :, 1]
            before = pltpu.roll(y[r * TW + 240 : r * TW + 256], 1, axis=0)
            even[hr, 0] = jnp.where(sub2 == 0, hcol[pl.ds(hr, 1), :], before).astype(BF16)
        return c

    lax.fori_loop(0, (TH + 1) // FIRST, first, 0)

    @pl.when(band_ref[0] == 0)
    def _():
        even[0] = jnp.zeros((9, 16, HID), BF16)
        odd[0] = jnp.zeros((8, 16, HID), BF16)

    fetches[6].wait()

    def second(step, c):
        lhs = jnp.concatenate(
            [
                jnp.concatenate(
                    [
                        x.reshape(128, HID)
                        for a in range(3)
                        for x in (
                            even[2 * (SECOND * step + r) + a, 0:8],
                            odd[2 * (SECOND * step + r) + a],
                            even[2 * (SECOND * step + r) + a, 1:9],
                        )
                    ],
                    axis=1,
                )
                for r in range(SECOND)
            ],
            axis=0,
        )
        y = gelu(jnp.dot(lhs, w2_ref[...], preferred_element_type=F32))
        for r in range(SECOND):
            for h in range(2):
                for t in range(8):
                    o32[r, h, pl.ds(t, 16, stride=8), :] = y[
                        r * 128 + t * 16 : r * 128 + (t + 1) * 16, h * 128 : (h + 1) * 128
                    ]
            out_ref[SECOND * step + r] = jnp.concatenate([o32[r, 0], o32[r, 1]], axis=1).astype(BF16)
        rows = pl.ds(SECOND * step, SECOND)
        pltpu.make_async_copy(out_ref.at[rows], out_hbm.at[rows], sem_out.at[step]).start()
        return c

    lax.fori_loop(0, TH // 2 // SECOND, second, 0)
    for i in range(TH // 2 // SECOND):
        rows = pl.ds(SECOND * i, SECOND)
        pltpu.make_async_copy(out_ref.at[rows], out_hbm.at[rows], sem_out.at[i]).wait()


def convolve(band, cells, north, south, own, west, east, w1, w2):
    return pl.pallas_call(
        conv_kernel,
        out_shape=jax.ShapeDtypeStruct((TH // 2, TW // 2, HID), BF16),
        in_specs=[pl.BlockSpec(memory_space=pltpu.SMEM)] + [pl.BlockSpec(memory_space=pl.ANY)] * 8,
        out_specs=pl.BlockSpec(memory_space=pl.ANY),
        scratch_shapes=[
            pltpu.VMEM((TH + 3, 18, 16, CH), BF16),
            pltpu.VMEM((TH + 1, 9, 16, HID), BF16),
            pltpu.VMEM((TH + 1, 8, 16, HID), BF16),
            pltpu.VMEM((COLS, CH), BF16),
            pltpu.VMEM((2, COLS, CH), BF16),
            pltpu.VMEM((COLS, CH), BF16),
            pltpu.VMEM((COLS, CH), F32),
            pltpu.VMEM((COLS, CH), F32),
            pltpu.VMEM((40, HID), F32),
            pltpu.VMEM((9 * CH, HID), BF16),
            pltpu.VMEM((9 * HID, HID), BF16),
            pltpu.VMEM((SECOND, 2, TW // 2, 128), F32),
            pltpu.VMEM((TH // 2, TW // 2, HID), BF16),
            pltpu.SemaphoreType.DMA((7 + (TH + 1) // FIRST,)),
            pltpu.SemaphoreType.DMA((TH // 2 // SECOND,)),
        ],
        compiler_params=pltpu.CompilerParams(vmem_limit_bytes=52 * 1024 * 1024),
        name="convolve",
    )(
        band, cells.reshape(TH, 16, 16, CH), north.reshape(2, 16, 16, CH), south.reshape(16, 16, CH),
        own, west, east, w1, w2,
    )


def body(obs_values, obs_dest, obs_cell, obs_count, conv_in, conv_down):
    lat = lax.axis_size("lat")
    lon = lax.axis_size("lon")
    send = pack(obs_values, obs_dest, obs_cell, obs_count)
    got = lax.all_to_all(
        send.reshape(DEV, BLK // 2, 2, CH), ("lat", "lon"), split_axis=0, concat_axis=0, tiled=True
    )
    cells, top, bottom, edge = to_grid(got.reshape(SEND, CH))
    north = lax.ppermute(bottom, "lat", [(i, i + 1) for i in range(lat - 1)])
    south = lax.ppermute(top, "lat", [(i + 1, i) for i in range(lat - 1)])
    north3 = north.reshape(2, TW, CH)
    full = jnp.stack(
        [
            jnp.concatenate(
                [north3[:, at], edge[e], south[at : at + 1], jnp.zeros((COLS - TH - 3, CH), BF16)]
            )
            for e, at in enumerate((0, 239, 255))
        ]
    )
    own = full[0]
    west = lax.ppermute(full[1:], "lon", [(i, (i + 1) % lon) for i in range(lon)])
    east = lax.ppermute(own, "lon", [((i + 1) % lon, i) for i in range(lon)])
    band = lax.axis_index("lat").astype(jnp.int32).reshape(1)
    return convolve(
        band, cells, north, south, own, west, east,
        conv_in.reshape(9 * CH, HID), conv_down.reshape(9 * HID, HID),
    )


def solution(mesh):
    placed = (
        P(("lat", "lon"), None),
        P(("lat", "lon"), None),
        P(("lat", "lon")),
        P(("lat", "lon")),
        P(),
        P(),
    )
    return jax.shard_map(
        body, mesh=mesh, in_specs=placed, out_specs=P("lat", "lon", None), check_vma=False
    )
```

```python
import functools

import jax
import jax.numpy as jnp
from jax import lax
from jax.experimental import pallas as pl
from jax.experimental.pallas import tpu as pltpu
from jax.sharding import PartitionSpec as P

TH = 32
TW = 256
CH = 128
HID = 256
DEV = 128
CAP = 64
ROWS = 4096
BLK = 66
SEND = DEV * BLK
TRASH = 256
GROUP = 8
FIRST = 11
SECOND = 8
COLS = 48
F32 = jnp.float32
BF16 = jnp.bfloat16


def gelu(x):
    inner = x * (0.7978845608028654 + 0.035677408136300125 * (x * x))
    return (0.5 * x) * (1.0 + jnp.tanh(inner))


def pack_kernel(
    count_ref, dest_hbm, cell_hbm, val_hbm, out_hbm,
    dest_ref, cell_ref, val_ref, o16, x32, o32, slot_v, slot_s, sem, sem_in, sem_out,
):
    fetches = [
        pltpu.make_async_copy(src, dst, sem_in.at[i])
        for i, (src, dst) in enumerate(((dest_hbm, dest_ref), (cell_hbm, cell_ref), (val_hbm, val_ref)))
    ]
    for fetch in fetches:
        fetch.start()
    count = count_ref[0]
    lane = lax.broadcasted_iota(jnp.int32, (1, 256), 1)
    dest_ids = lax.broadcasted_iota(jnp.int32, (DEV, 256), 0)
    pos_ids = lax.broadcasted_iota(jnp.int32, (CAP, 256), 0)
    upper = (
        lax.broadcasted_iota(jnp.int32, (256, 256), 0)
        < lax.broadcasted_iota(jnp.int32, (256, 256), 1)
    ).astype(F32).astype(BF16)
    fetches[0].wait()
    fetches[1].wait()
    carry = jnp.zeros((DEV, 1), F32)
    cells = jnp.zeros((DEV, 2 * CAP), F32)
    slots = []
    for a in range(ROWS // 256):
        dest = jnp.concatenate([dest_ref[2 * a : 2 * a + 1], dest_ref[2 * a + 1 : 2 * a + 2]], axis=1)
        cell = jnp.concatenate([cell_ref[2 * a : 2 * a + 1], cell_ref[2 * a + 1 : 2 * a + 2]], axis=1)
        live = (lane + 256 * a) < count
        dest_or = jnp.where(live, dest, DEV)
        hot = (dest_ids == dest_or).astype(F32)
        hot16 = hot.astype(BF16)
        before = jnp.dot(hot16, upper, preferred_element_type=F32) + carry
        carry = carry + jnp.sum(hot, axis=1, keepdims=True)
        pos = jnp.sum(hot * before, axis=0, keepdims=True).astype(jnp.int32)
        slot = jnp.where(live, dest * BLK + pos, SEND)
        slots += [slot[:, :128], slot[:, 128:]]
        high = (cell // TW + 1).astype(F32)
        low = ((cell % 16) * 16 + (cell % TW) // 16).astype(F32)
        pos_hot = pos_ids == pos
        coded = jnp.concatenate(
            [jnp.where(pos_hot, high, 0.0), jnp.where(pos_hot, low, 0.0)], axis=0
        ).astype(BF16)
        cells = cells + lax.dot_general(
            hot16, coded, (((1,), (1,)), ((), ())), preferred_element_type=F32
        )
    slot_v[...] = jnp.concatenate(slots, axis=0)
    to_scalar = pltpu.make_async_copy(slot_v, slot_s, sem)
    to_scalar.start()
    fetches[2].wait()

    def widen(i, c):
        rows = pl.ds(pl.multiple_of(i * 128, 128), 128)
        x32[rows, :] = val_ref[rows, :].astype(F32)
        return c

    lax.fori_loop(0, ROWS // 128, widen, 0)
    to_scalar.wait()

    def move(i, c):
        for k in range(ROWS // 128):
            o32[pl.ds(slot_s.at[k][i], 1), :] = x32[pl.ds(k * 128 + i, 1), :]
        return c

    lax.fori_loop(0, 128, move, 0)
    for d in range(DEV):
        o32[d * BLK + CAP : d * BLK + CAP + 1, :] = cells[d : d + 1, :]

    def narrow(i, c):
        rows = pl.ds(pl.multiple_of(i * 128, 128), 128)
        o16[rows, :] = o32[rows, :].astype(BF16)
        return c

    parts = 3
    stores = []
    for p in range(parts):
        lax.fori_loop(p * SEND // 128 // parts, (p + 1) * SEND // 128 // parts, narrow, 0)
        rows = pl.ds(p * SEND // parts, SEND // parts)
        store = pltpu.make_async_copy(o16.at[rows], out_hbm.at[rows], sem_out.at[p])
        store.start()
        stores.append(store)
    for store in stores:
        store.wait()


def pack(obs_values, obs_dest, obs_cell, obs_count):
    return pl.pallas_call(
        pack_kernel,
        out_shape=jax.ShapeDtypeStruct((SEND, CH), BF16),
        in_specs=[pl.BlockSpec(memory_space=pltpu.SMEM)] + [pl.BlockSpec(memory_space=pl.ANY)] * 3,
        out_specs=pl.BlockSpec(memory_space=pl.ANY),
        scratch_shapes=[
            pltpu.VMEM((32, 128), jnp.int32),
            pltpu.VMEM((32, 128), jnp.int32),
            pltpu.VMEM((ROWS, CH), BF16),
            pltpu.VMEM((SEND, CH), BF16),
            pltpu.VMEM((ROWS, CH), F32),
            pltpu.VMEM((SEND + 8, CH), F32),
            pltpu.VMEM((32, 128), jnp.int32),
            pltpu.SMEM((32, 128), jnp.int32),
            pltpu.SemaphoreType.DMA,
            pltpu.SemaphoreType.DMA((3,)),
            pltpu.SemaphoreType.DMA((3,)),
        ],
        compiler_params=pltpu.CompilerParams(vmem_limit_bytes=60 * 1024 * 1024),
        name="pack",
    )(obs_count, obs_dest.reshape(32, 128), obs_cell.reshape(32, 128), obs_values)


def grid_kernel(
    got_hbm, out_hbm, top_ref, bottom_ref, edge_ref,
    got_ref, out_ref, x32, acc, acc2, table_v, table_s, rowpair, colpair, inverse, edge32, sem, sem_in, sem_out,
):
    parts = 4
    fetches = []
    for p in range(parts):
        rows = pl.ds(p * SEND // parts, SEND // parts)
        fetch = pltpu.make_async_copy(got_hbm.at[rows], got_ref.at[rows], sem_in.at[p])
        fetch.start()
        fetches.append(fetch)

    def clear(i, c):
        acc[pl.ds(pl.multiple_of(i * 128, 128), 128), :] = jnp.zeros((128, CH), F32)
        acc2[pl.ds(pl.multiple_of(i * 128, 128), 128), :] = jnp.zeros((128, CH), F32)
        return c

    lax.fori_loop(0, (TRASH + TH * TW) // 128, clear, 0)

    def widen(i, c):
        rows = pl.ds(pl.multiple_of(i * 192, 192), 192)
        x32[rows, :] = got_ref[rows, :].astype(F32)
        return c

    for p in range(parts):
        fetches[p].wait()
        lax.fori_loop(p * SEND // 192 // parts, (p + 1) * SEND // 192 // parts, widen, 0)
    cells = x32[pl.ds(CAP, DEV, stride=BLK), :]
    swapped = pltpu.roll(cells, CAP, axis=1)
    lane = lax.broadcasted_iota(jnp.int32, (DEV, 128), 1)
    first = lane < CAP
    index = jnp.where(
        cells == 0.0, lane, cells.astype(jnp.int32) * TW + swapped.astype(jnp.int32)
    )
    index = jnp.where(first, index, -1)
    repeated = jnp.zeros((DEV, 128), jnp.bool_)
    for d in range(1, GROUP):
        same = (index == pltpu.roll(index, d, axis=1)) & (lane % GROUP >= d)
        repeated = repeated | same
    repeated = jnp.where(first & repeated, 1.0, 0.0).astype(BF16)
    slot = lax.broadcasted_iota(jnp.int32, (128, 128), 0)
    kind = lax.broadcasted_iota(jnp.int32, (128, 128), 1) - CAP
    groups = ((kind == 0) | (slot // GROUP == kind - 8)).astype(F32).astype(BF16)
    flags = jnp.dot(repeated, groups, preferred_element_type=F32)
    flags = (flags + pltpu.roll(flags, DEV // 2, axis=0)).astype(jnp.int32)
    table_v[...] = jnp.where(first, index, flags).T
    to_scalar = []
    for n, rows in enumerate((pl.ds(CAP, 16), pl.ds(0, CAP))):
        to_scalar.append(pltpu.make_async_copy(table_v.at[rows], table_s.at[rows], sem.at[n]))
        to_scalar[n].start()

    half = DEV // 2
    firsth = lax.broadcasted_iota(jnp.int32, (half, 128), 1) < CAP
    rowpair[...] = jnp.where(firsth, cells[:half], swapped[half:])
    colpair[...] = jnp.where(firsth, swapped[:half], cells[half:])
    batch = 16
    col_ids = lax.broadcasted_iota(jnp.int32, (TW, 128), 0).astype(F32)
    row_ids = (lax.broadcasted_iota(jnp.int32, (128, 128), 0) + 1).astype(F32)

    def tally(i, total):
        at = [pl.ds(i * batch + k, 1) for k in range(batch)]
        col_hot = jnp.concatenate(
            [(col_ids == colpair[r, :]).astype(F32).astype(BF16) for r in at], axis=1
        )
        row_hot = jnp.concatenate(
            [(row_ids == rowpair[r, :]).astype(F32).astype(BF16) for r in at], axis=1
        )
        return total + lax.dot_general(
            col_hot, row_hot, (((1,), (1,)), ((), ())), preferred_element_type=F32
        )

    tallies = lax.fori_loop(0, half // batch, tally, jnp.zeros((TW, 128), F32))
    inverse[...] = 1.0 / jnp.maximum(tallies, 1.0)

    to_scalar[0].wait()
    to_scalar[1].wait()

    def source(s, c):
        pairs = ((acc, s), (acc2, s + half))

        def add_group(g):
            slots = range(g * GROUP, (g + 1) * GROUP)
            index = [[pl.ds(table_s.at[k][t], 1) for k in slots] for _, t in pairs]
            sums = [
                [a[at, :] + x32[pl.ds(t * BLK + k, 1), :] for at, k in zip(ix, slots)]
                for (a, t), ix in zip(pairs, index)
            ]
            for (a, _), ix, new in zip(pairs, index, sums):
                for at, value in zip(ix, new):
                    a[at, :] = value

        def add_singly(g):
            for k in range(g * GROUP, (g + 1) * GROUP):
                for a, t in pairs:
                    at = pl.ds(table_s.at[k][t], 1)
                    a[at, :] = a[at, :] + x32[pl.ds(t * BLK + k, 1), :]

        clash = table_s.at[CAP][s]

        @pl.when(clash == 0)
        def _():
            for g in range(CAP // GROUP):
                add_group(g)

        @pl.when(clash != 0)
        def _():
            for g in range(CAP // GROUP):
                here = table_s.at[CAP + 8 + g][s]
                pl.when(here == 0)(lambda: add_group(g))
                pl.when(here != 0)(lambda: add_singly(g))

        return c

    lax.fori_loop(0, half, source, 0)

    span = TH // parts

    def normalise(p, c):
        scales = inverse[...]
        for k in range(span):
            i = p * span + k
            rows = pl.ds(pl.multiple_of(TRASH + i * TW, TW), TW)
            mean = (acc[rows, :] + acc2[rows, :]) * jnp.broadcast_to(scales[:, k : k + 1], (TW, CH))
            out_ref[pl.ds(pl.multiple_of(i * TW, TW), TW), :] = mean.astype(BF16)
            for e, at in enumerate((0, 239, 255)):
                edge32[e, pl.ds(i, 1), :] = mean[at : at + 1]
        inverse[...] = pltpu.roll(scales, 128 - span, axis=1)
        rows = pl.ds(pl.multiple_of(p * span * TW, TW), span * TW)
        pltpu.make_async_copy(out_ref.at[rows], out_hbm.at[rows], sem_out.at[p]).start()
        return c

    lax.fori_loop(0, parts, normalise, 0)
    top_ref[...] = out_ref[:TW, :]
    bottom_ref[...] = out_ref[(TH - 2) * TW :, :]
    edge_ref[...] = edge32[...].astype(BF16)
    for p in range(parts):
        rows = pl.ds(p * span * TW, span * TW)
        pltpu.make_async_copy(out_ref.at[rows], out_hbm.at[rows], sem_out.at[p]).wait()


def to_grid(got):
    shapes = [(TH * TW, CH), (TW, CH), (2 * TW, CH), (3, TH, CH)]
    return pl.pallas_call(
        grid_kernel,
        out_shape=[jax.ShapeDtypeStruct(s, BF16) for s in shapes],
        in_specs=[pl.BlockSpec(memory_space=pl.ANY)],
        out_specs=[pl.BlockSpec(memory_space=pl.ANY)] + [pl.BlockSpec(memory_space=pltpu.VMEM)] * 3,
        scratch_shapes=[
            pltpu.VMEM((SEND, CH), BF16),
            pltpu.VMEM((TH * TW, CH), BF16),
            pltpu.VMEM((SEND, CH), F32),
            pltpu.VMEM((TRASH + TH * TW, CH), F32),
            pltpu.VMEM((TRASH + TH * TW, CH), F32),
            pltpu.VMEM((DEV, 128), jnp.int32),
            pltpu.SMEM((CAP + 16, 128), jnp.int32),
            pltpu.VMEM((DEV // 2, 128), F32),
            pltpu.VMEM((DEV // 2, 128), F32),
            pltpu.VMEM((TW, 128), F32),
            pltpu.VMEM((3, TH, CH), F32),
            pltpu.SemaphoreType.DMA((2,)),
            pltpu.SemaphoreType.DMA((4,)),
            pltpu.SemaphoreType.DMA((4,)),
        ],
        compiler_params=pltpu.CompilerParams(vmem_limit_bytes=52 * 1024 * 1024),
        name="to_grid",
    )(got)


def conv_kernel(
    band_ref, cell_hbm, north_hbm, south_hbm, own_hbm, west_hbm, east_hbm, w1_hbm, w2_hbm, out_hbm,
    field, even, odd, own_ref, west_ref, east_ref, wcol, ecol, hcol, w1_ref, w2_ref, o32, out_ref, sem, sem_out,
):
    steps = (TH + 1) // FIRST
    pairs = [
        (west_hbm, west_ref),
        (east_hbm, east_ref),
        (own_hbm, own_ref),
        (w1_hbm, w1_ref),
        (north_hbm, field.at[pl.ds(0, 2), pl.ds(1, 16)]),
        (south_hbm, field.at[2 + TH, pl.ds(1, 16)]),
        (w2_hbm, w2_ref),
    ]
    for i in range(steps):
        size = min(TH, (i + 1) * FIRST) - i * FIRST
        pairs.append(
            (cell_hbm.at[pl.ds(i * FIRST, size)], field.at[pl.ds(2 + i * FIRST, size), pl.ds(1, 16)])
        )
    fetches = [pltpu.make_async_copy(src, dst, sem.at[i]) for i, (src, dst) in enumerate(pairs)]
    for fetch in fetches:
        fetch.start()
    for fetch in fetches[:6]:
        fetch.wait()
    wcol[...] = west_ref[1].astype(F32)
    ecol[...] = east_ref[...].astype(F32)
    sub = lax.broadcasted_iota(jnp.int32, (16, CH), 0)

    def wrap(r, c):
        before = pltpu.roll(field[r, 16].astype(F32), 1, axis=0)
        field[r, 0] = jnp.where(sub == 0, wcol[pl.ds(r, 1), :], before).astype(BF16)
        after = pltpu.roll(field[r, 1].astype(F32), 15, axis=0)
        field[r, 17] = jnp.where(sub == 15, ecol[pl.ds(r, 1), :], after).astype(BF16)
        return c

    taps = [west_ref[0].astype(F32), west_ref[1].astype(F32), own_ref[...].astype(F32)]
    lhs = jnp.concatenate([taps[b][a : a + 40] for a in range(3) for b in range(3)], axis=1)
    hcol[...] = gelu(jnp.dot(lhs.astype(BF16), w1_ref[...], preferred_element_type=F32))
    lax.fori_loop(0, 2, wrap, 0)
    sub2 = lax.broadcasted_iota(jnp.int32, (16, HID), 0)

    def first(step, c):
        for i in range(steps):
            pl.when(step == i)(fetches[7 + i].wait)
        lax.fori_loop(2 + FIRST * step, 2 + FIRST * (step + 1), wrap, 0)
        lhs = jnp.concatenate(
            [
                field[pl.ds(FIRST * step + a, FIRST), b : b + 16].reshape(FIRST * TW, CH)
                for a in range(3)
                for b in range(3)
            ],
            axis=1,
        )
        y = gelu(jnp.dot(lhs, w1_ref[...], preferred_element_type=F32))
        y16 = y.astype(BF16).reshape(FIRST, 8, 2, 16, HID)
        for r in range(FIRST):
            hr = FIRST * step + r
            odd[hr] = y16[r, :, 0]
            even[hr, 1:9] = y16[r, :, 1]
            before = pltpu.roll(y[r * TW + 240 : r * TW + 256], 1, axis=0)
            even[hr, 0] = jnp.where(sub2 == 0, hcol[pl.ds(hr, 1), :], before).astype(BF16)
        return c

    lax.fori_loop(0, (TH + 1) // FIRST, first, 0)

    @pl.when(band_ref[0] == 0)
    def _():
        even[0] = jnp.zeros((9, 16, HID), BF16)
        odd[0] = jnp.zeros((8, 16, HID), BF16)

    fetches[6].wait()

    def second(step, c):
        lhs = jnp.concatenate(
            [
                jnp.concatenate(
                    [
                        x.reshape(128, HID)
                        for a in range(3)
                        for x in (
                            even[2 * (SECOND * step + r) + a, 0:8],
                            odd[2 * (SECOND * step + r) + a],
                            even[2 * (SECOND * step + r) + a, 1:9],
                        )
                    ],
                    axis=1,
                )
                for r in range(SECOND)
            ],
            axis=0,
        )
        y = gelu(jnp.dot(lhs, w2_ref[...], preferred_element_type=F32))
        for r in range(SECOND):
            for h in range(2):
                for t in range(8):
                    o32[r, h, pl.ds(t, 16, stride=8), :] = y[
                        r * 128 + t * 16 : r * 128 + (t + 1) * 16, h * 128 : (h + 1) * 128
                    ]
            out_ref[SECOND * step + r] = jnp.concatenate([o32[r, 0], o32[r, 1]], axis=1).astype(BF16)
        rows = pl.ds(SECOND * step, SECOND)
        pltpu.make_async_copy(out_ref.at[rows], out_hbm.at[rows], sem_out.at[step]).start()
        return c

    lax.fori_loop(0, TH // 2 // SECOND, second, 0)
    for i in range(TH // 2 // SECOND):
        rows = pl.ds(SECOND * i, SECOND)
        pltpu.make_async_copy(out_ref.at[rows], out_hbm.at[rows], sem_out.at[i]).wait()


def convolve(band, cells, north, south, own, west, east, w1, w2):
    return pl.pallas_call(
        conv_kernel,
        out_shape=jax.ShapeDtypeStruct((TH // 2, TW // 2, HID), BF16),
        in_specs=[pl.BlockSpec(memory_space=pltpu.SMEM)] + [pl.BlockSpec(memory_space=pl.ANY)] * 8,
        out_specs=pl.BlockSpec(memory_space=pl.ANY),
        scratch_shapes=[
            pltpu.VMEM((TH + 3, 18, 16, CH), BF16),
            pltpu.VMEM((TH + 1, 9, 16, HID), BF16),
            pltpu.VMEM((TH + 1, 8, 16, HID), BF16),
            pltpu.VMEM((COLS, CH), BF16),
            pltpu.VMEM((2, COLS, CH), BF16),
            pltpu.VMEM((COLS, CH), BF16),
            pltpu.VMEM((COLS, CH), F32),
            pltpu.VMEM((COLS, CH), F32),
            pltpu.VMEM((40, HID), F32),
            pltpu.VMEM((9 * CH, HID), BF16),
            pltpu.VMEM((9 * HID, HID), BF16),
            pltpu.VMEM((SECOND, 2, TW // 2, 128), F32),
            pltpu.VMEM((TH // 2, TW // 2, HID), BF16),
            pltpu.SemaphoreType.DMA((7 + (TH + 1) // FIRST,)),
            pltpu.SemaphoreType.DMA((TH // 2 // SECOND,)),
        ],
        compiler_params=pltpu.CompilerParams(vmem_limit_bytes=52 * 1024 * 1024),
        name="convolve",
    )(
        band, cells.reshape(TH, 16, 16, CH), north.reshape(2, 16, 16, CH), south.reshape(16, 16, CH),
        own, west, east, w1, w2,
    )


def body(obs_values, obs_dest, obs_cell, obs_count, conv_in, conv_down):
    lat = lax.axis_size("lat")
    lon = lax.axis_size("lon")
    send = pack(obs_values, obs_dest, obs_cell, obs_count)
    got = lax.all_to_all(
        send.reshape(DEV, BLK // 2, 2, CH), ("lat", "lon"), split_axis=0, concat_axis=0, tiled=True
    )
    cells, top, bottom, edge = to_grid(got.reshape(SEND, CH))
    north = lax.ppermute(bottom, "lat", [(i, i + 1) for i in range(lat - 1)])
    south = lax.ppermute(top, "lat", [(i + 1, i) for i in range(lat - 1)])
    north3 = north.reshape(2, TW, CH)
    full = jnp.stack(
        [
            jnp.concatenate(
                [north3[:, at], edge[e], south[at : at + 1], jnp.zeros((COLS - TH - 3, CH), BF16)]
            )
            for e, at in enumerate((0, 239, 255))
        ]
    )
    own = full[0]
    west = lax.ppermute(full[1:], "lon", [(i, (i + 1) % lon) for i in range(lon)])
    east = lax.ppermute(own, "lon", [((i + 1) % lon, i) for i in range(lon)])
    band = lax.axis_index("lat").astype(jnp.int32).reshape(1)
    return convolve(
        band, cells, north, south, own, west, east,
        conv_in.reshape(9 * CH, HID), conv_down.reshape(9 * HID, HID),
    )


def solution(mesh):
    placed = (
        P(("lat", "lon"), None),
        P(("lat", "lon"), None),
        P(("lat", "lon")),
        P(("lat", "lon")),
        P(),
        P(),
    )
    return jax.shard_map(
        body, mesh=mesh, in_specs=placed, out_specs=P("lat", "lon", None), check_vma=False
    )
```

```python
import functools

import jax
import jax.numpy as jnp
from jax import lax
from jax.experimental import pallas as pl
from jax.experimental.pallas import tpu as pltpu
from jax.sharding import PartitionSpec as P

TH = 32
TW = 256
CH = 128
HID = 256
DEV = 128
CAP = 64
ROWS = 4096
BLK = 66
SEND = DEV * BLK
TRASH = 256
GROUP = 8
FIRST = 11
SECOND = 8
COLS = 48
F32 = jnp.float32
BF16 = jnp.bfloat16


def gelu(x):
    inner = x * (0.7978845608028654 + 0.035677408136300125 * (x * x))
    return (0.5 * x) * (1.0 + jnp.tanh(inner))


def pack_kernel(
    count_ref, dest_hbm, cell_hbm, val_hbm, out_hbm,
    dest_ref, cell_ref, val_ref, o16, x32, o32, slot_v, slot_s, sem, sem_in, sem_out,
):
    fetches = [
        pltpu.make_async_copy(src, dst, sem_in.at[i])
        for i, (src, dst) in enumerate(((dest_hbm, dest_ref), (cell_hbm, cell_ref), (val_hbm, val_ref)))
    ]
    for fetch in fetches:
        fetch.start()
    count = count_ref[0]
    lane = lax.broadcasted_iota(jnp.int32, (1, 256), 1)
    dest_ids = lax.broadcasted_iota(jnp.int32, (DEV, 256), 0)
    pos_ids = lax.broadcasted_iota(jnp.int32, (CAP, 256), 0)
    upper = (
        lax.broadcasted_iota(jnp.int32, (256, 256), 0)
        < lax.broadcasted_iota(jnp.int32, (256, 256), 1)
    ).astype(F32).astype(BF16)
    fetches[0].wait()
    fetches[1].wait()
    carry = jnp.zeros((DEV, 1), F32)
    cells = jnp.zeros((DEV, 2 * CAP), F32)
    slots = []
    for a in range(ROWS // 256):
        dest = jnp.concatenate([dest_ref[2 * a : 2 * a + 1], dest_ref[2 * a + 1 : 2 * a + 2]], axis=1)
        cell = jnp.concatenate([cell_ref[2 * a : 2 * a + 1], cell_ref[2 * a + 1 : 2 * a + 2]], axis=1)
        live = (lane + 256 * a) < count
        dest_or = jnp.where(live, dest, DEV)
        hot = (dest_ids == dest_or).astype(F32)
        hot16 = hot.astype(BF16)
        before = jnp.dot(hot16, upper, preferred_element_type=F32) + carry
        carry = carry + jnp.sum(hot, axis=1, keepdims=True)
        pos = jnp.sum(hot * before, axis=0, keepdims=True).astype(jnp.int32)
        slot = jnp.where(live, dest * BLK + pos, SEND)
        slots += [slot[:, :128], slot[:, 128:]]
        high = (cell // TW + 1).astype(F32)
        low = ((cell % 16) * 16 + (cell % TW) // 16).astype(F32)
        pos_hot = pos_ids == pos
        coded = jnp.concatenate(
            [jnp.where(pos_hot, high, 0.0), jnp.where(pos_hot, low, 0.0)], axis=0
        ).astype(BF16)
        cells = cells + lax.dot_general(
            hot16, coded, (((1,), (1,)), ((), ())), preferred_element_type=F32
        )
    slot_v[...] = jnp.concatenate(slots, axis=0)
    to_scalar = pltpu.make_async_copy(slot_v, slot_s, sem)
    to_scalar.start()
    fetches[2].wait()

    def widen(i, c):
        rows = pl.ds(pl.multiple_of(i * 128, 128), 128)
        x32[rows, :] = val_ref[rows, :].astype(F32)
        return c

    lax.fori_loop(0, ROWS // 128, widen, 0)
    to_scalar.wait()

    def move(i, c):
        for k in range(ROWS // 128):
            o32[pl.ds(slot_s.at[k][i], 1), :] = x32[pl.ds(k * 128 + i, 1), :]
        return c

    lax.fori_loop(0, 128, move, 0)
    for d in range(DEV):
        o32[d * BLK + CAP : d * BLK + CAP + 1, :] = cells[d : d + 1, :]

    def narrow(i, c):
        rows = pl.ds(pl.multiple_of(i * 128, 128), 128)
        o16[rows, :] = o32[rows, :].astype(BF16)
        return c

    parts = 3
    stores = []
    for p in range(parts):
        lax.fori_loop(p * SEND // 128 // parts, (p + 1) * SEND // 128 // parts, narrow, 0)
        rows = pl.ds(p * SEND // parts, SEND // parts)
        store = pltpu.make_async_copy(o16.at[rows], out_hbm.at[rows], sem_out.at[p])
        store.start()
        stores.append(store)
    for store in stores:
        store.wait()


def pack(obs_values, obs_dest, obs_cell, obs_count):
    return pl.pallas_call(
        pack_kernel,
        out_shape=jax.ShapeDtypeStruct((SEND, CH), BF16),
        in_specs=[pl.BlockSpec(memory_space=pltpu.SMEM)] + [pl.BlockSpec(memory_space=pl.ANY)] * 3,
        out_specs=pl.BlockSpec(memory_space=pl.ANY),
        scratch_shapes=[
            pltpu.VMEM((32, 128), jnp.int32),
            pltpu.VMEM((32, 128), jnp.int32),
            pltpu.VMEM((ROWS, CH), BF16),
            pltpu.VMEM((SEND, CH), BF16),
            pltpu.VMEM((ROWS, CH), F32),
            pltpu.VMEM((SEND + 8, CH), F32),
            pltpu.VMEM((32, 128), jnp.int32),
            pltpu.SMEM((32, 128), jnp.int32),
            pltpu.SemaphoreType.DMA,
            pltpu.SemaphoreType.DMA((3,)),
            pltpu.SemaphoreType.DMA((3,)),
        ],
        compiler_params=pltpu.CompilerParams(vmem_limit_bytes=60 * 1024 * 1024),
        name="pack",
    )(obs_count, obs_dest.reshape(32, 128), obs_cell.reshape(32, 128), obs_values)


def grid_kernel(
    got_hbm, out_hbm, top_ref, bottom_ref, edge_ref,
    got_ref, out_ref, x32, acc, acc2, table_v, table_s, rowpair, colpair, inverse, edge32, sem, sem_in, sem_out,
):
    parts = 4
    fetches = []
    for p in range(parts):
        rows = pl.ds(p * SEND // parts, SEND // parts)
        fetch = pltpu.make_async_copy(got_hbm.at[rows], got_ref.at[rows], sem_in.at[p])
        fetch.start()
        fetches.append(fetch)

    def clear(i, c):
        acc[pl.ds(pl.multiple_of(i * 128, 128), 128), :] = jnp.zeros((128, CH), F32)
        acc2[pl.ds(pl.multiple_of(i * 128, 128), 128), :] = jnp.zeros((128, CH), F32)
        return c

    lax.fori_loop(0, (TRASH + TH * TW) // 128, clear, 0)

    def widen(i, c):
        rows = pl.ds(pl.multiple_of(i * 192, 192), 192)
        x32[rows, :] = got_ref[rows, :].astype(F32)
        return c

    for p in range(parts):
        fetches[p].wait()
        lax.fori_loop(p * SEND // 192 // parts, (p + 1) * SEND // 192 // parts, widen, 0)
    cells = x32[pl.ds(CAP, DEV, stride=BLK), :]
    swapped = pltpu.roll(cells, CAP, axis=1)
    lane = lax.broadcasted_iota(jnp.int32, (DEV, 128), 1)
    first = lane < CAP
    index = jnp.where(
        cells == 0.0, lane, cells.astype(jnp.int32) * TW + swapped.astype(jnp.int32)
    )
    index = jnp.where(first, index, -1)
    repeated = jnp.zeros((DEV, 128), jnp.bool_)
    for d in range(1, GROUP):
        same = (index == pltpu.roll(index, d, axis=1)) & (lane % GROUP >= d)
        repeated = repeated | same
    repeated = jnp.where(first & repeated, 1.0, 0.0).astype(BF16)
    slot = lax.broadcasted_iota(jnp.int32, (128, 128), 0)
    kind = lax.broadcasted_iota(jnp.int32, (128, 128), 1) - CAP
    groups = ((kind == 0) | (slot // GROUP == kind - 8)).astype(F32).astype(BF16)
    flags = jnp.dot(repeated, groups, preferred_element_type=F32)
    flags = (flags + pltpu.roll(flags, DEV // 2, axis=0)).astype(jnp.int32)
    table_v[...] = jnp.where(first, index, flags).T
    to_scalar = []
    for n, rows in enumerate((pl.ds(CAP, 16), pl.ds(0, CAP))):
        to_scalar.append(pltpu.make_async_copy(table_v.at[rows], table_s.at[rows], sem.at[n]))
        to_scalar[n].start()

    half = DEV // 2
    firsth = lax.broadcasted_iota(jnp.int32, (half, 128), 1) < CAP
    rowpair[...] = jnp.where(firsth, cells[:half], swapped[half:])
    colpair[...] = jnp.where(firsth, swapped[:half], cells[half:])
    batch = 32
    col_ids = lax.broadcasted_iota(jnp.int32, (TW, 128), 0).astype(F32)
    row_ids = (lax.broadcasted_iota(jnp.int32, (128, 128), 0) + 1).astype(F32)

    def tally(i, total):
        at = [pl.ds(i * batch + k, 1) for k in range(batch)]
        col_hot = jnp.concatenate(
            [(col_ids == colpair[r, :]).astype(F32).astype(BF16) for r in at], axis=1
        )
        row_hot = jnp.concatenate(
            [(row_ids == rowpair[r, :]).astype(F32).astype(BF16) for r in at], axis=1
        )
        return total + lax.dot_general(
            col_hot, row_hot, (((1,), (1,)), ((), ())), preferred_element_type=F32
        )

    tallies = lax.fori_loop(0, half // batch, tally, jnp.zeros((TW, 128), F32))
    inverse[...] = 1.0 / jnp.maximum(tallies, 1.0)

    to_scalar[0].wait()
    to_scalar[1].wait()

    def source(s, c):
        pairs = ((acc, s), (acc2, s + half))

        def add_group(g):
            slots = range(g * GROUP, (g + 1) * GROUP)
            index = [[pl.ds(table_s.at[k][t], 1) for k in slots] for _, t in pairs]
            sums = [
                [a[at, :] + x32[pl.ds(t * BLK + k, 1), :] for at, k in zip(ix, slots)]
                for (a, t), ix in zip(pairs, index)
            ]
            for (a, _), ix, new in zip(pairs, index, sums):
                for at, value in zip(ix, new):
                    a[at, :] = value

        def add_singly(g):
            for k in range(g * GROUP, (g + 1) * GROUP):
                for a, t in pairs:
                    at = pl.ds(table_s.at[k][t], 1)
                    a[at, :] = a[at, :] + x32[pl.ds(t * BLK + k, 1), :]

        clash = table_s.at[CAP][s]

        @pl.when(clash == 0)
        def _():
            for g in range(CAP // GROUP):
                add_group(g)

        @pl.when(clash != 0)
        def _():
            for g in range(CAP // GROUP):
                here = table_s.at[CAP + 8 + g][s]
                pl.when(here == 0)(lambda: add_group(g))
                pl.when(here != 0)(lambda: add_singly(g))

        return c

    lax.fori_loop(0, half, source, 0)

    span = TH // parts

    def normalise(p, c):
        scales = inverse[...]
        for k in range(span):
            i = p * span + k
            rows = pl.ds(pl.multiple_of(TRASH + i * TW, TW), TW)
            mean = (acc[rows, :] + acc2[rows, :]) * jnp.broadcast_to(scales[:, k : k + 1], (TW, CH))
            out_ref[pl.ds(pl.multiple_of(i * TW, TW), TW), :] = mean.astype(BF16)
            for e, at in enumerate((0, 239, 255)):
                edge32[e, pl.ds(i, 1), :] = mean[at : at + 1]
        inverse[...] = pltpu.roll(scales, 128 - span, axis=1)
        rows = pl.ds(pl.multiple_of(p * span * TW, TW), span * TW)
        pltpu.make_async_copy(out_ref.at[rows], out_hbm.at[rows], sem_out.at[p]).start()
        return c

    lax.fori_loop(0, parts, normalise, 0)
    top_ref[...] = out_ref[:TW, :]
    bottom_ref[...] = out_ref[(TH - 2) * TW :, :]
    edge_ref[...] = edge32[...].astype(BF16)
    for p in range(parts):
        rows = pl.ds(p * span * TW, span * TW)
        pltpu.make_async_copy(out_ref.at[rows], out_hbm.at[rows], sem_out.at[p]).wait()


def to_grid(got):
    shapes = [(TH * TW, CH), (TW, CH), (2 * TW, CH), (3, TH, CH)]
    return pl.pallas_call(
        grid_kernel,
        out_shape=[jax.ShapeDtypeStruct(s, BF16) for s in shapes],
        in_specs=[pl.BlockSpec(memory_space=pl.ANY)],
        out_specs=[pl.BlockSpec(memory_space=pl.ANY)] + [pl.BlockSpec(memory_space=pltpu.VMEM)] * 3,
        scratch_shapes=[
            pltpu.VMEM((SEND, CH), BF16),
            pltpu.VMEM((TH * TW, CH), BF16),
            pltpu.VMEM((SEND, CH), F32),
            pltpu.VMEM((TRASH + TH * TW, CH), F32),
            pltpu.VMEM((TRASH + TH * TW, CH), F32),
            pltpu.VMEM((DEV, 128), jnp.int32),
            pltpu.SMEM((CAP + 16, 128), jnp.int32),
            pltpu.VMEM((DEV // 2, 128), F32),
            pltpu.VMEM((DEV // 2, 128), F32),
            pltpu.VMEM((TW, 128), F32),
            pltpu.VMEM((3, TH, CH), F32),
            pltpu.SemaphoreType.DMA((2,)),
            pltpu.SemaphoreType.DMA((4,)),
            pltpu.SemaphoreType.DMA((4,)),
        ],
        compiler_params=pltpu.CompilerParams(vmem_limit_bytes=52 * 1024 * 1024),
        name="to_grid",
    )(got)


def conv_kernel(
    band_ref, cell_hbm, north_hbm, south_hbm, own_hbm, west_hbm, east_hbm, w1_hbm, w2_hbm, out_hbm,
    field, even, odd, own_ref, west_ref, east_ref, wcol, ecol, hcol, w1_ref, w2_ref, o32, out_ref, sem, sem_out,
):
    steps = (TH + 1) // FIRST
    pairs = [
        (west_hbm, west_ref),
        (east_hbm, east_ref),
        (own_hbm, own_ref),
        (w1_hbm, w1_ref),
        (north_hbm, field.at[pl.ds(0, 2), pl.ds(1, 16)]),
        (south_hbm, field.at[2 + TH, pl.ds(1, 16)]),
        (w2_hbm, w2_ref),
    ]
    for i in range(steps):
        size = min(TH, (i + 1) * FIRST) - i * FIRST
        pairs.append(
            (cell_hbm.at[pl.ds(i * FIRST, size)], field.at[pl.ds(2 + i * FIRST, size), pl.ds(1, 16)])
        )
    fetches = [pltpu.make_async_copy(src, dst, sem.at[i]) for i, (src, dst) in enumerate(pairs)]
    for fetch in fetches:
        fetch.start()
    for fetch in fetches[:6]:
        fetch.wait()
    wcol[...] = west_ref[1].astype(F32)
    ecol[...] = east_ref[...].astype(F32)
    sub = lax.broadcasted_iota(jnp.int32, (16, CH), 0)

    def wrap(r, c):
        before = pltpu.roll(field[r, 16].astype(F32), 1, axis=0)
        field[r, 0] = jnp.where(sub == 0, wcol[pl.ds(r, 1), :], before).astype(BF16)
        after = pltpu.roll(field[r, 1].astype(F32), 15, axis=0)
        field[r, 17] = jnp.where(sub == 15, ecol[pl.ds(r, 1), :], after).astype(BF16)
        return c

    taps = [west_ref[0].astype(F32), west_ref[1].astype(F32), own_ref[...].astype(F32)]
    lhs = jnp.concatenate([taps[b][a : a + 40] for a in range(3) for b in range(3)], axis=1)
    hcol[...] = gelu(jnp.dot(lhs.astype(BF16), w1_ref[...], preferred_element_type=F32))
    lax.fori_loop(0, 2, wrap, 0)
    sub2 = lax.broadcasted_iota(jnp.int32, (16, HID), 0)

    def first(step, c):
        for i in range(steps):
            pl.when(step == i)(fetches[7 + i].wait)
        lax.fori_loop(2 + FIRST * step, 2 + FIRST * (step + 1), wrap, 0)
        lhs = jnp.concatenate(
            [
                field[pl.ds(FIRST * step + a, FIRST), b : b + 16].reshape(FIRST * TW, CH)
                for a in range(3)
                for b in range(3)
            ],
            axis=1,
        )
        y = gelu(jnp.dot(lhs, w1_ref[...], preferred_element_type=F32))
        y16 = y.astype(BF16).reshape(FIRST, 8, 2, 16, HID)
        for r in range(FIRST):
            hr = FIRST * step + r
            odd[hr] = y16[r, :, 0]
            even[hr, 1:9] = y16[r, :, 1]
            before = pltpu.roll(y[r * TW + 240 : r * TW + 256], 1, axis=0)
            even[hr, 0] = jnp.where(sub2 == 0, hcol[pl.ds(hr, 1), :], before).astype(BF16)
        return c

    lax.fori_loop(0, (TH + 1) // FIRST, first, 0)

    @pl.when(band_ref[0] == 0)
    def _():
        even[0] = jnp.zeros((9, 16, HID), BF16)
        odd[0] = jnp.zeros((8, 16, HID), BF16)

    fetches[6].wait()

    def second(step, c):
        lhs = jnp.concatenate(
            [
                jnp.concatenate(
                    [
                        x.reshape(128, HID)
                        for a in range(3)
                        for x in (
                            even[2 * (SECOND * step + r) + a, 0:8],
                            odd[2 * (SECOND * step + r) + a],
                            even[2 * (SECOND * step + r) + a, 1:9],
                        )
                    ],
                    axis=1,
                )
                for r in range(SECOND)
            ],
            axis=0,
        )
        y = gelu(jnp.dot(lhs, w2_ref[...], preferred_element_type=F32))
        for r in range(SECOND):
            for h in range(2):
                for t in range(8):
                    o32[r, h, pl.ds(t, 16, stride=8), :] = y[
                        r * 128 + t * 16 : r * 128 + (t + 1) * 16, h * 128 : (h + 1) * 128
                    ]
            out_ref[SECOND * step + r] = jnp.concatenate([o32[r, 0], o32[r, 1]], axis=1).astype(BF16)
        rows = pl.ds(SECOND * step, SECOND)
        pltpu.make_async_copy(out_ref.at[rows], out_hbm.at[rows], sem_out.at[step]).start()
        return c

    lax.fori_loop(0, TH // 2 // SECOND, second, 0)
    for i in range(TH // 2 // SECOND):
        rows = pl.ds(SECOND * i, SECOND)
        pltpu.make_async_copy(out_ref.at[rows], out_hbm.at[rows], sem_out.at[i]).wait()


def convolve(band, cells, north, south, own, west, east, w1, w2):
    return pl.pallas_call(
        conv_kernel,
        out_shape=jax.ShapeDtypeStruct((TH // 2, TW // 2, HID), BF16),
        in_specs=[pl.BlockSpec(memory_space=pltpu.SMEM)] + [pl.BlockSpec(memory_space=pl.ANY)] * 8,
        out_specs=pl.BlockSpec(memory_space=pl.ANY),
        scratch_shapes=[
            pltpu.VMEM((TH + 3, 18, 16, CH), BF16),
            pltpu.VMEM((TH + 1, 9, 16, HID), BF16),
            pltpu.VMEM((TH + 1, 8, 16, HID), BF16),
            pltpu.VMEM((COLS, CH), BF16),
            pltpu.VMEM((2, COLS, CH), BF16),
            pltpu.VMEM((COLS, CH), BF16),
            pltpu.VMEM((COLS, CH), F32),
            pltpu.VMEM((COLS, CH), F32),
            pltpu.VMEM((40, HID), F32),
            pltpu.VMEM((9 * CH, HID), BF16),
            pltpu.VMEM((9 * HID, HID), BF16),
            pltpu.VMEM((SECOND, 2, TW // 2, 128), F32),
            pltpu.VMEM((TH // 2, TW // 2, HID), BF16),
            pltpu.SemaphoreType.DMA((7 + (TH + 1) // FIRST,)),
            pltpu.SemaphoreType.DMA((TH // 2 // SECOND,)),
        ],
        compiler_params=pltpu.CompilerParams(vmem_limit_bytes=52 * 1024 * 1024),
        name="convolve",
    )(
        band, cells.reshape(TH, 16, 16, CH), north.reshape(2, 16, 16, CH), south.reshape(16, 16, CH),
        own, west, east, w1, w2,
    )


def body(obs_values, obs_dest, obs_cell, obs_count, conv_in, conv_down):
    lat = lax.axis_size("lat")
    lon = lax.axis_size("lon")
    send = pack(obs_values, obs_dest, obs_cell, obs_count)
    got = lax.all_to_all(
        send.reshape(DEV, BLK // 2, 2, CH), ("lat", "lon"), split_axis=0, concat_axis=0, tiled=True
    )
    cells, top, bottom, edge = to_grid(got.reshape(SEND, CH))
    north = lax.ppermute(bottom, "lat", [(i, i + 1) for i in range(lat - 1)])
    south = lax.ppermute(top, "lat", [(i + 1, i) for i in range(lat - 1)])
    north3 = north.reshape(2, TW, CH)
    full = jnp.stack(
        [
            jnp.concatenate(
                [north3[:, at], edge[e], south[at : at + 1], jnp.zeros((COLS - TH - 3, CH), BF16)]
            )
            for e, at in enumerate((0, 239, 255))
        ]
    )
    own = full[0]
    west = lax.ppermute(full[1:], "lon", [(i, (i + 1) % lon) for i in range(lon)])
    east = lax.ppermute(own, "lon", [((i + 1) % lon, i) for i in range(lon)])
    band = lax.axis_index("lat").astype(jnp.int32).reshape(1)
    return convolve(
        band, cells, north, south, own, west, east,
        conv_in.reshape(9 * CH, HID), conv_down.reshape(9 * HID, HID),
    )


def solution(mesh):
    placed = (
        P(("lat", "lon"), None),
        P(("lat", "lon"), None),
        P(("lat", "lon")),
        P(("lat", "lon")),
        P(),
        P(),
    )
    return jax.shard_map(
        body, mesh=mesh, in_specs=placed, out_specs=P("lat", "lon", None), check_vma=False
    )
```
